32 devices in a mesh: row: 8 (over y, x, core), col: 4 (over z).
Axes of the slice: x: 2, y: 2, z: 4, core: 2. Of those that a mesh axis runs over, the one named last changes fastest.
Arguments:
- frames: bfloat16 [2, 64, 64, 512], P(None, None, 'row', 'col'), may hold values from -6 to 6
- state: bfloat16 [64, 64, 512], P(None, 'row', 'col'), may hold values from -1 to 1
- input_weight: bfloat16 [9, 192, 64], replicated, may hold values from -0.25 to 0.25
- state_weight: bfloat16 [9, 192, 64], replicated, may hold values from -0.25 to 0.25
- cotangent: bfloat16 [64, 64, 512], P(None, 'row', 'col'), may hold values from -6 to 6
Outputs:
- final_state: bfloat16 [64, 64, 512], P(None, 'row', 'col')
- grad_state: float32 [64, 64, 512], P(None, 'row', 'col')
- grad_input_weights: float32 [9, 192, 64], replicated
- grad_state_weights: float32 [9, 192, 64], replicated
The draws below stay inside these ranges and needn't reach their ends.
All inputs are finite; a program needn't handle non-finite values.
Results may differ from the reference program's by a relative error of at most 0.0048.
Values may be sent and summed in bfloat16 or wider, within the bound.
No kernel may reach another device: no remote copies, remote signals or barrier semaphores. Data moves between devices by JAX's collectives and lax.ppermute only.
A program may use at most 64 MiB of HBM per device.

```python
import jax
import jax.numpy as jnp
from jax import lax

C = 64
CI = 64
STEPS = 2
NY = 64
NX = 512


def levels(rng, dims, cuts, smallest, high):
    factor_of, own = 1.0, jax.random.fold_in(rng, 6)
    for dim, blocks in cuts:
        heights = jnp.exp(jax.random.uniform(jax.random.fold_in(own, dim), (blocks,), jnp.float32, smallest / len(cuts), high / len(cuts)))
        factor_of = factor_of * jnp.repeat(heights, dims[dim] // blocks).reshape([-1 if axis == dim else 1 for axis in range(len(dims))])
    return factor_of


def noise(rng, dims, scale, most, split=(), dtype=jnp.bfloat16):
    level = levels(rng, dims, split, -0.22, 0.18) if split else 1.0
    result = jax.random.normal(rng, dims, jnp.float32) * scale * level
    return jnp.minimum(jnp.maximum(result, -most), most).astype(dtype)


def setup_inputs(seed: int = 0) -> dict:
    key_list = jax.random.split(jax.random.key(seed), 6)
    return {
        "frames": noise(key_list[0], (STEPS, CI, NY, NX), 1.0, 6.0, ((2, 8), (3, 4))),
        "state": jnp.clip(jax.random.uniform(key_list[1], (C, NY, NX), jnp.float32, -1.0, 1.0) * levels(key_list[1], (C, NY, NX), ((1, 8), (2, 4)), -0.4, 0.0), -1.0, 1.0).astype(jnp.bfloat16),
        "input_weight": noise(key_list[2], (9, 3 * C, CI), (9 * CI) ** -0.5, 0.25),
        "state_weight": noise(key_list[3], (9, 3 * C, C), (9 * C) ** -0.5, 0.25),
        "cotangent": noise(key_list[4], (C, NY, NX), 1.0, 6.0, ((1, 8), (2, 4))),
    }


def conv_taps(weights, padded, out_rows, out_cols):
    running = None
    for tap_index in range(9):
        window = padded[:, tap_index // 3:tap_index // 3 + out_rows, tap_index % 3:tap_index % 3 + out_cols]
        flattened = window.reshape(window.shape[0], out_rows * out_cols)
        product = jnp.dot(weights[tap_index], flattened, preferred_element_type=jnp.float32)
        running = product if running is None else running + product
    return running.reshape(weights.shape[1], out_rows, out_cols)

def gate_fields(frame_pad, state_pad, input_weight, state_weight, out_rows, out_cols):
    channels = state_weight.shape[2]
    from_input = conv_taps(input_weight, frame_pad, out_rows, out_cols)
    from_state = conv_taps(state_weight, state_pad, out_rows, out_cols)
    previous = state_pad[:, 1:-1, 1:-1].astype(jnp.float32)
    update = jax.nn.sigmoid(from_input[:channels] + from_state[:channels])
    reset_gate = jax.nn.sigmoid(from_input[channels:2 * channels] + from_state[channels:2 * channels])
    state_term = from_state[2 * channels:]
    candidate = jnp.tanh(from_input[2 * channels:] + reset_gate * state_term)
    new_state = ((1.0 - update) * candidate + update * previous).astype(jnp.bfloat16)
    return (new_state, (update, reset_gate, candidate, state_term))

def gate_grads(grad_state, saved, previous):
    update, reset_gate, candidate, state_term = saved
    grad_candidate = grad_state * (1.0 - update)
    grad_update = grad_state * (previous.astype(jnp.float32) - candidate)
    pre_update = grad_update * update * (1.0 - update)
    pre_candidate = grad_candidate * (1.0 - candidate * candidate)
    pre_reset = pre_candidate * state_term * reset_gate * (1.0 - reset_gate)
    pre_hidden = pre_candidate * reset_gate
    input_pre = jnp.concatenate([pre_update, pre_reset, pre_candidate], 0).astype(jnp.bfloat16)
    state_pre = jnp.concatenate([pre_update, pre_reset, pre_hidden], 0).astype(jnp.bfloat16)
    return (input_pre, state_pre, grad_state * update)

def weight_grad(pre_grad, padded, out_rows, out_cols):
    flat_pre = pre_grad.reshape(pre_grad.shape[0], out_rows * out_cols)
    pieces = []
    for tap_index in range(9):
        window = padded[:, tap_index // 3:tap_index // 3 + out_rows, tap_index % 3:tap_index % 3 + out_cols]
        flattened = window.reshape(window.shape[0], out_rows * out_cols)
        pieces.append(lax.dot_general(flat_pre, flattened, (((1,), (1,)), ((), ())), preferred_element_type=jnp.float32))
    return jnp.stack(pieces, 0)

def spread_back(weights, pre_grad, out_rows, out_cols):
    flat_pre = pre_grad.reshape(pre_grad.shape[0], out_rows * out_cols)
    padded = jnp.zeros((weights.shape[2], out_rows + 2, out_cols + 2), jnp.float32)
    for tap_index in range(9):
        product = lax.dot_general(weights[tap_index], flat_pre, (((0,), (0,)), ((), ())), preferred_element_type=jnp.float32)
        start_row = tap_index // 3
        start_col = tap_index % 3
        padded = padded.at[:, start_row:start_row + out_rows, start_col:start_col + out_cols].add(product.reshape(weights.shape[2], out_rows, out_cols))
    return padded

def pad_field(field_value):
    return jnp.pad(field_value, ((0, 0), (1, 1), (1, 1)))

def reference(frames, state, input_weight, state_weight, cotangent):
    step_count = frames.shape[0]
    rows = state.shape[1]
    cols = state.shape[2]
    records = []
    current = state
    for step_index in range(step_count):
        frame_pad = pad_field(frames[step_index])
        state_pad = pad_field(current)
        new_state, saved = gate_fields(frame_pad, state_pad, input_weight, state_weight, rows, cols)
        records.append((frame_pad, state_pad, saved))
        current = new_state
    grad_state = cotangent.astype(jnp.float32)
    input_sum = jnp.zeros(input_weight.shape, jnp.float32)
    state_sum = jnp.zeros(state_weight.shape, jnp.float32)
    for step_index in reversed(range(step_count)):
        frame_pad, state_pad, saved = records[step_index]
        input_pre, state_pre, direct = gate_grads(grad_state, saved, state_pad[:, 1:-1, 1:-1])
        input_sum = input_sum + weight_grad(input_pre, frame_pad, rows, cols)
        state_sum = state_sum + weight_grad(state_pre, state_pad, rows, cols)
        spread = spread_back(state_weight, state_pre, rows, cols)[:, 1:-1, 1:-1]
        grad_state = direct + spread
    loss_scale = (rows * cols) ** (-0.5)
    return (current, grad_state, input_sum * loss_scale, state_sum * loss_scale)
```

```python
import functools

import jax
import jax.numpy as jnp
from jax import lax
from jax.experimental import pallas as pl
from jax.experimental.pallas import tpu as pltpu
from jax.sharding import PartitionSpec as P

F32 = jnp.float32
BF16 = jnp.bfloat16

HALO = 4
EDGE = 8
GAP = 2 * EDGE


def mosaic_params(limit):
    return pltpu.CompilerParams(vmem_limit_bytes=limit)


def pack_kernel(tr, tc, frames, state, cot, own, left, right, rows_f32):
    ch = state.shape[0]
    fields = (frames[0], state[...], frames[1], cot[...])
    for f, v in enumerate(fields):
        rows_f32[f] = v.astype(F32).reshape(ch * tr, tc)
    lefts, rights = [], []
    for r in range(tr):
        rows = [rows_f32[f, pl.ds(r, ch, stride=tr), :] for f in range(4)]
        a = jnp.concatenate(rows[:2], 0).T
        b = jnp.concatenate(rows[2:], 0).T
        ab = jnp.concatenate([a, b], 1)
        own[r * tc : (r + 1) * tc, :] = ab.astype(BF16)
        lefts.append(ab[:EDGE])
        rights.append(ab[tc - EDGE :])
    left[...] = jnp.concatenate(lefts, 0).astype(BF16)
    right[...] = jnp.concatenate(rights, 0).astype(BF16)


def pack(frames, state, cot):
    ch, tr, tc = state.shape
    return pl.pallas_call(
        functools.partial(pack_kernel, tr, tc),
        out_shape=(
            jax.ShapeDtypeStruct((tr * tc, 4 * ch), BF16),
            jax.ShapeDtypeStruct((tr * EDGE, 4 * ch), BF16),
            jax.ShapeDtypeStruct((tr * EDGE, 4 * ch), BF16),
        ),
        scratch_shapes=[pltpu.VMEM((4, ch * tr, tc), F32)],
        compiler_params=mosaic_params(24 * 2**20),
        cost_estimate=pl.CostEstimate(flops=0, bytes_accessed=1200000, transcendentals=0),
        name="pack",
    )(frames, state, cot)


def main_kernel(
    tr, tc, nrow, ncol, flat_rows,
    own, hl, hr, nb_core, nb_far, wf, wb,
    final_ref, grad_ref, mine_ref, send_ref,
    x1, x2, f2, xd, p, o, ru1, t1, direct, mask, dw, tmp,
):
    pitch = tc + GAP
    ext = tr + 2 * HALO
    total = xd.shape[1]
    pad = 8
    row = lax.axis_index("row")
    col = lax.axis_index("col")
    parity = lax.rem(row, 2)
    lane_low = lax.broadcasted_iota(jnp.int32, (1, 128), 1) < 64

    z8 = jnp.zeros((8, 128), F32)
    for ref in (x1, f2, x2):
        ref[0 : pad + 8, :] = jnp.zeros((pad + 8, 128), F32)
        tail = ref.shape[0] - (pad + ext * pitch + 8)
        ref[pad + ext * pitch + 8 :, :] = jnp.zeros((tail, 128), F32)

    def place(start, cells, lft, rgt, count):
        for i in range(count):
            at = (start + i) * pitch + pad
            if not isinstance(start, int):
                at = pl.multiple_of(at, 8)
            for ref, lanes in ((x1, slice(0, 128)), (f2, slice(128, 256))):
                ref[pl.ds(at + GAP, tc), :] = cells[i * tc : (i + 1) * tc, lanes]
                ref[pl.ds(at + EDGE, EDGE), :] = lft[i * EDGE : (i + 1) * EDGE, lanes]
                ref[pl.ds(at + pitch, EDGE), :] = rgt[i * EDGE : (i + 1) * EDGE, lanes]

    place(HALO, own[...].astype(F32), hl[...].astype(F32), hr[...].astype(F32), tr)
    a, b = HALO * tc, HALO * EDGE
    for ref, start in ((nb_core, (1 - parity) * (HALO + tr)), (nb_far, parity * (HALO + tr))):
        v = ref[...].astype(F32)
        place(start, v[:a], v[a : a + b], v[a + b :], HALO)

    mask[0:8, :] = z8
    tail = mask.shape[0] - (ext * pitch + 8)
    mask[ext * pitch + 8 :, :] = jnp.zeros((tail, 128), F32)
    has_left = (col > 0).astype(F32)
    has_right = (col < ncol - 1).astype(F32)
    for r in range(ext):
        if r < HALO:
            ok = (row > 0).astype(F32)
        elif r >= HALO + tr:
            ok = (row < nrow - 1).astype(F32)
        else:
            ok = jnp.float32(1.0)
        at = r * pitch
        mask[at + EDGE : at + GAP, :] = jnp.full((EDGE, 128), ok * has_left, F32)
        mask[at + GAP : at + pitch, :] = jnp.full((tc, 128), ok, F32)
        mask[at + pitch : at + pitch + EDGE, :] = jnp.full((EDGE, 128), ok * has_right, F32)

    def spread_columns(src, t):
        step = 288
        for n in range(0, total, step):
            m = min(step, total - n)
            for dx in range(3):
                xd[t, n : n + m, dx * 128 : (dx + 1) * 128] = src[
                    pad + n + dx - 1 : pad + n + dx - 1 + m, :
                ].astype(BF16)

    def gates(t, n, m):
        g = None
        for dy in range(3):
            at = n + (dy - 1) * pitch
            d = jnp.dot(
                xd[t, at : at + m, :],
                wf[dy * 384 : (dy + 1) * 384, :],
                preferred_element_type=F32,
            )
            g = d if g is None else g + d
        g1, g2 = g[:, :128], g[:, 128:]
        ru = 0.5 * jnp.tanh(0.5 * g1) + 0.5
        c = jnp.tanh(g2 + pltpu.roll(ru * g2, 64, 1))
        return ru, jnp.where(lane_low, g2, c)

    def pre_grads(g, s, ru, tt):
        om = 1.0 - ru
        pc = g * om * (1.0 - tt * tt)
        ph = pltpu.roll(pc, 64, 1) * ru
        pa = jnp.where(lane_low, ph * tt, g * (s - tt) * ru) * om
        pb = jnp.where(lane_low, ph, pc)
        return pa.astype(BF16), pb.astype(BF16)

    spread_columns(x1, 0)
    first = pitch
    m = 256
    count = -(-((ext - 2) * pitch + GAP) // m)
    for i in range(count):
        n = first + i * m
        ru, tt = gates(0, n, m)
        s = x1[pad + n : pad + n + m, :]
        new = (tt + ru * (s - tt)) * mask[n : n + m, :]
        new = new.astype(BF16).astype(F32)
        x2[pad + n : pad + n + m, :] = jnp.where(lane_low, f2[pad + n : pad + n + m, :], new)
        ru1[n : n + m, :] = ru
        t1[n : n + m, :] = tt
    done = first + count * m
    x2[pad + done :, :] = jnp.zeros((x2.shape[0] - pad - done, 128), F32)
    x2[pad + 8 : pad + first, :] = jnp.zeros((first - 8, 128), F32)

    spread_columns(x2, 1)
    first = 2 * pitch
    count = -(-((ext - 4) * pitch + GAP) // m)
    p[0:first, :] = jnp.zeros((first, 256), BF16)
    done = first + count * m
    p[done:, :] = jnp.zeros((p.shape[0] - done, 256), BF16)
    for i in range(count):
        n = first + i * m
        ru, tt = gates(1, n, m)
        s = x2[pad + n : pad + n + m, :]
        o[n : n + m, 0:128] = tt + ru * (s - tt)
        g = f2[pad + n : pad + n + m, :]
        pa, pb = pre_grads(g, s, ru, tt)
        p[n : n + m, 0:128] = pa
        p[n : n + m, 128:256] = pb
        direct[n : n + m, :] = g * ru
    ch = 64
    for r in range(tr):
        at = (HALO + r) * pitch + GAP
        tmp[pl.ds(r, ch, stride=tr), :] = o[at : at + tc, 0:128].T[64:, :]
    final_ref[...] = tmp[...].reshape(ch, tr, tc).astype(BF16)

    def weight_grads(t, add):
        pt = jnp.concatenate(
            [
                p[(HALO + r) * pitch + GAP : (HALO + r) * pitch + GAP + tc, :].T
                for r in range(tr)
            ],
            1,
        )
        for dy in range(3):
            at = [(HALO + r + dy - 1) * pitch + GAP for r in range(tr)]
            x = jnp.concatenate([xd[t, k : k + tc, :] for k in at], 0)
            d = jnp.dot(pt, x, preferred_element_type=F32)
            dw[dy] = dw[dy] + d if add else d

    def back_data(first, size, step):
        n = first
        while n < first + size:
            m = min(step, first + size - n)
            acc = None
            for dy in range(3):
                at = n - (dy - 1) * pitch
                d = jnp.dot(
                    p[at : at + m, :],
                    wb[dy * 256 : (dy + 1) * 256, :],
                    preferred_element_type=F32,
                )
                acc = d if acc is None else acc + d
            o[n : n + m, :] = acc
            n += m

    def gathered(n, m):
        return (
            pltpu.roll(o[n + 1 : n + 1 + m, 0:128], 64, 1)
            + o[n : n + m, 0:128]
            + o[n - 1 : n - 1 + m, 128:256]
        )

    weight_grads(1, False)
    back_data(3 * pitch - 16, (ext - 6) * pitch + 2 * GAP + 96, 256)

    first = 3 * pitch
    count = -(-((ext - 6) * pitch + GAP) // m)
    for i in range(count):
        n = first + i * m
        g = (direct[n : n + m, :] + gathered(n, m)) * mask[n : n + m, :]
        ru = ru1[n : n + m, :]
        pa, pb = pre_grads(g, x1[pad + n : pad + n + m, :], ru, t1[n : n + m, :])
        p[n : n + m, 0:128] = pa
        p[n : n + m, 128:256] = pb
        direct[n : n + m, :] = g * ru
    weight_grads(0, True)
    back_data(HALO * pitch, tr * pitch + GAP, 256)
    for r in range(tr):
        at = (HALO + r) * pitch + GAP
        g = direct[at : at + tc, :] + gathered(at, tc)
        grad_ref[pl.ds(r, ch, stride=tr), :] = g.T[64:, :]

    half = flat_rows // 2
    flat = o
    for tap in range(9):
        dy, dx = tap // 3, tap % 3
        d = dw[dy, :, dx * 128 : (dx + 1) * 128]
        at = tap * 192
        flat[at : at + 128, 0:128] = d[:128]
        flat[at + 128 : at + 192, 0:128] = jnp.where(lane_low, d[192:256], d[128:192])
    if flat_rows > 9 * 192:
        flat[9 * 192 : flat_rows, 0:128] = jnp.zeros((flat_rows - 9 * 192, 128), F32)
    mine_ref[...] = flat[pl.ds(pl.multiple_of(parity * half, 16), half), 0:128]
    send_ref[...] = flat[pl.ds(pl.multiple_of((1 - parity) * half, 16), half), 0:128].astype(BF16)


def main(own, hl, hr, nb_core, nb_far, wf, wb, ch, tr, tc, flat_rows):
    nrow, ncol = lax.axis_size("row"), lax.axis_size("col")
    pitch = tc + GAP
    ext = tr + 2 * HALO
    cells = (ext + 1) * pitch + GAP
    cells = -(-cells // 16) * 16
    o_rows = max(cells, flat_rows)
    half = flat_rows // 2
    return pl.pallas_call(
        functools.partial(main_kernel, tr, tc, nrow, ncol, flat_rows),
        out_shape=(
            jax.ShapeDtypeStruct((ch, tr, tc), BF16),
            jax.ShapeDtypeStruct((ch * tr, tc), F32),
            jax.ShapeDtypeStruct((half, 128), F32),
            jax.ShapeDtypeStruct((half, 128), BF16),
        ),
        scratch_shapes=[
            pltpu.VMEM((cells + 16, 128), F32),
            pltpu.VMEM((cells + 16, 128), F32),
            pltpu.VMEM((cells + 16, 128), F32),
            pltpu.VMEM((2, cells, 384), BF16),
            pltpu.VMEM((cells, 256), BF16),
            pltpu.VMEM((o_rows, 256), F32),
            pltpu.VMEM((cells, 128), F32),
            pltpu.VMEM((cells, 128), F32),
            pltpu.VMEM((cells, 128), F32),
            pltpu.VMEM((cells, 128), F32),
            pltpu.VMEM((3, 256, 384), F32),
            pltpu.VMEM((ch * tr, tc), F32),
        ],
        compiler_params=mosaic_params(48 * 2**20),
        cost_estimate=pl.CostEstimate(flops=3000000000, bytes_accessed=4000000, transcendentals=600000),
        name="steps",
    )(own, hl, hr, nb_core, nb_far, wf, wb)


def reduce_kernel(scale, parts, out):
    total = parts[0].astype(F32)
    for i in range(1, parts.shape[0]):
        total = total + parts[i].astype(F32)
    v = (total * scale).astype(BF16)
    for i in range(parts.shape[0]):
        out[i] = v


def reduce_parts(parts, scale):
    return pl.pallas_call(
        functools.partial(reduce_kernel, scale),
        out_shape=jax.ShapeDtypeStruct(parts.shape, BF16),
        compiler_params=mosaic_params(16 * 2**20),
        name="reduce_parts",
    )(parts)


def unpack_kernel(mine, other, gi, gs, flat):
    half = mine.shape[0]
    parity = lax.rem(lax.axis_index("row"), 2)
    flat[pl.ds(pl.multiple_of(parity * half, 16), half), :] = mine[...].astype(F32)
    flat[pl.ds(pl.multiple_of((1 - parity) * half, 16), half), :] = other[...].astype(F32)
    for tap in range(9):
        at = tap * 192
        for to, frm in ((0, 64), (64, 0), (128, 128)):
            v = flat[at + frm : at + frm + 64, :]
            gi[tap, to : to + 64, :] = v[:, :64]
            gs[tap, to : to + 64, :] = v[:, 64:]


def unpack(mine, other, shape):
    return pl.pallas_call(
        unpack_kernel,
        out_shape=(jax.ShapeDtypeStruct(shape, F32), jax.ShapeDtypeStruct(shape, F32)),
        scratch_shapes=[pltpu.VMEM((2 * mine.shape[0], 128), F32)],
        compiler_params=mosaic_params(24 * 2**20),
        name="unpack",
    )(mine, other)


def arrange_weights(iw, sw):
    ch = sw.shape[2]
    z = jnp.zeros((9, ch, ch), BF16)
    it, st = jnp.swapaxes(iw, 1, 2), jnp.swapaxes(sw, 1, 2)
    u, r, c = slice(0, ch), slice(ch, 2 * ch), slice(2 * ch, 3 * ch)
    from_frame = jnp.concatenate([it[:, :, r], it[:, :, u], z, it[:, :, c]], 2)
    from_state = jnp.concatenate([st[:, :, r], st[:, :, u], st[:, :, c], z], 2)
    wf = jnp.concatenate([from_frame, from_state], 1).reshape(9 * 2 * ch, 4 * ch)
    back = jnp.concatenate([sw[:, r], sw[:, u], sw[:, c], z], 1).reshape(3, 3, 4 * ch, ch)
    zb = jnp.zeros((3, 4 * ch, ch), BF16)
    wb = jnp.concatenate([back[:, 0], back[:, 1], zb, back[:, 2]], 2).reshape(3 * 4 * ch, 4 * ch)
    return wf, wb


def local(frames, state, input_weight, state_weight, cotangent):
    ch, tr, tc = state.shape
    nrow, ncol = lax.axis_size("row"), lax.axis_size("col")
    ndev = nrow * ncol
    parity = lax.rem(lax.axis_index("row"), 2)

    own, left, right = pack(frames, state, cotangent)
    hr = lax.ppermute(left, "col", [(i, i - 1) for i in range(1, ncol)])
    hl = lax.ppermute(right, "col", [(i, i + 1) for i in range(ncol - 1)])
    wf, wb = arrange_weights(input_weight, state_weight)

    def row_block(first):
        cut = lambda v, w: lax.dynamic_slice_in_dim(v, first * w, HALO * w, 0)
        return jnp.concatenate([cut(own, tc), cut(hl, EDGE), cut(hr, EDGE)], 0)

    core_pairs = [(i, i ^ 1) for i in range(nrow)]
    far_pairs = []
    for i in range(1, nrow - 1, 2):
        far_pairs += [(i, i + 1), (i + 1, i)]
    nb_far = lax.ppermute(row_block(parity * (tr - HALO)), "row", far_pairs)
    nb_core = lax.ppermute(row_block((1 - parity) * (tr - HALO)), "row", core_pairs)

    chunk = -(-9 * 192 // ndev)
    chunk = -(-chunk // 16) * 16
    final, grad, mine, send = main(
        own, hl, hr, nb_core, nb_far, wf, wb, ch, tr, tc, chunk * ndev
    )
    got = lax.ppermute(send, "row", core_pairs)
    both = (mine + got.astype(F32)).astype(BF16).reshape(ndev // 2, chunk, 128)
    groups = [
        [r * ncol + c for r in range(core, nrow, 2) for c in range(ncol)] for core in range(2)
    ]
    parts = lax.all_to_all(both, ("row", "col"), 0, 0, axis_index_groups=groups)
    scale = float((tr * nrow * tc * ncol) ** (-0.5))
    sums = reduce_parts(parts, scale)
    whole = lax.all_to_all(sums, ("row", "col"), 0, 0, axis_index_groups=groups)
    whole = whole.reshape(ndev // 2 * chunk, 128)
    other = lax.ppermute(whole, "row", core_pairs)
    gi, gs = unpack(whole, other, input_weight.shape)
    return final, grad.reshape(ch, tr, tc), gi, gs


def solution(mesh):
    in_specs = (P(None, None, "row", "col"), P(None, "row", "col"), P(), P(), P(None, "row", "col"))
    out_specs = (P(None, "row", "col"), P(None, "row", "col"), P(), P())
    return jax.shard_map(local, mesh=mesh, in_specs=in_specs, out_specs=out_specs, check_vma=False)
```

```python
import functools

import jax
import jax.numpy as jnp
from jax import lax
from jax.experimental import pallas as pl
from jax.experimental.pallas import tpu as pltpu
from jax.sharding import PartitionSpec as P

F32 = jnp.float32
BF16 = jnp.bfloat16

HALO = 4
EDGE = 8
GAP = 2 * EDGE


def mosaic_params(limit):
    return pltpu.CompilerParams(vmem_limit_bytes=limit)


def pack_kernel(
    tr, tc, frames_hbm, state_hbm, cot_hbm,
    corners, to_core, to_far_1, to_far_2, own, left, right,
    frames, state, cot, rows_f32, sems,
):
    copies = [
        pltpu.make_async_copy(src, dst, sems.at[i])
        for i, (src, dst) in enumerate(
            ((frames_hbm.at[0], frames.at[0]), (state_hbm, state), (frames_hbm.at[1], frames.at[1]), (cot_hbm, cot))
        )
    ]
    for c in copies:
        c.start()
    ch = state.shape[0]
    fields = (frames.at[0], state, frames.at[1], cot)
    for f, v in enumerate(fields):
        copies[f].wait()
        rows_f32[f] = v[...].astype(F32).reshape(ch * tr, tc)
    lefts, rights = [], []
    for r in range(tr):
        rows = [rows_f32[f, pl.ds(r, ch, stride=tr), :] for f in range(4)]
        a = jnp.concatenate(rows[:2], 0).T
        b = jnp.concatenate(rows[2:], 0).T
        ab = jnp.concatenate([a, b], 1)
        own[r * tc : (r + 1) * tc, :] = ab.astype(BF16)
        lefts.append(ab[:EDGE])
        rights.append(ab[tc - EDGE :])
    left[...] = jnp.concatenate(lefts, 0).astype(BF16)
    right[...] = jnp.concatenate(rights, 0).astype(BF16)
    parity = lax.rem(lax.axis_index("row"), 2)
    block = HALO * tc
    last = (tr - HALO) * tc
    near = pl.multiple_of((1 - parity) * last, 16)
    far = pl.multiple_of(parity * last, 16)
    to_core[...] = own[pl.ds(near, block), :]
    to_far_1[...] = own[pl.ds(far, block), 0:128]
    to_far_2[...] = own[pl.ds(pl.multiple_of(far + parity * tc, 16), block - tc), 128:256]
    edge = pl.multiple_of(parity * (tr - HALO) * EDGE, 16)
    corners[0 : HALO * EDGE, :] = left[pl.ds(edge, HALO * EDGE), :]
    corners[HALO * EDGE :, :] = right[pl.ds(edge, HALO * EDGE), :]


def pack(frames, state, cot):
    ch, tr, tc = state.shape
    hbm = pl.BlockSpec(memory_space=pltpu.HBM)
    edge = jax.ShapeDtypeStruct((tr * EDGE, 4 * ch), BF16)
    return pl.pallas_call(
        functools.partial(pack_kernel, tr, tc),
        in_specs=[hbm, hbm, hbm],
        out_shape=(
            jax.ShapeDtypeStruct((2 * HALO * EDGE, 4 * ch), BF16),
            jax.ShapeDtypeStruct((HALO * tc, 4 * ch), BF16),
            jax.ShapeDtypeStruct((HALO * tc, 2 * ch), BF16),
            jax.ShapeDtypeStruct(((HALO - 1) * tc, 2 * ch), BF16),
            jax.ShapeDtypeStruct((tr * tc, 4 * ch), BF16),
            edge,
            edge,
        ),
        scratch_shapes=[
            pltpu.VMEM(frames.shape, BF16),
            pltpu.VMEM(state.shape, BF16),
            pltpu.VMEM(cot.shape, BF16),
            pltpu.VMEM((4, ch * tr, tc), F32),
            pltpu.SemaphoreType.DMA((4,)),
        ],
        compiler_params=mosaic_params(24 * 2**20),
        name="pack",
    )(frames, state, cot)


def edges_kernel(tr, tc, corners, core, left, right, a, b):
    n = HALO * EDGE
    nb = core[...].astype(F32)
    far = corners[...].astype(F32)
    lefts = [nb[i * tc : i * tc + EDGE] for i in range(HALO)]
    rights = [nb[(i + 1) * tc - EDGE : (i + 1) * tc] for i in range(HALO)]
    lft = jnp.concatenate([left[...].astype(F32)] + lefts + [far[:n]], 0)
    rgt = jnp.concatenate([right[...].astype(F32)] + rights + [far[n:]], 0)
    even = lax.rem(lax.axis_index("col"), 2) == 0
    a[...] = jnp.where(even, rgt, lft).astype(BF16)
    b[...] = jnp.where(even, lft, rgt).astype(BF16)


def edges(corners, core, left, right, tr, tc):
    shape = jax.ShapeDtypeStruct(((tr + 2 * HALO) * EDGE, left.shape[1]), BF16)
    return pl.pallas_call(
        functools.partial(edges_kernel, tr, tc),
        out_shape=(shape, shape),
        compiler_params=mosaic_params(16 * 2**20),
        name="edges",
    )(corners, core, left, right)


def weights_kernel(iw, sw, wf, wb):
    z = jnp.zeros((64, 64), F32)
    for tap in range(9):
        i, s = iw[tap].astype(F32), sw[tap].astype(F32)
        u, r, c = slice(0, 64), slice(64, 128), slice(128, 192)
        at = tap * 128
        wf[at : at + 64, :] = jnp.concatenate([i[:, r], i[:, u], z, i[:, c]], 1).astype(BF16)
        wf[at + 64 : at + 128, :] = jnp.concatenate([s[:, r], s[:, u], s[:, c], z], 1).astype(BF16)
    for dy in range(3):
        back = []
        for dx in range(3):
            s = sw[3 * dy + dx].astype(F32)
            back.append(jnp.concatenate([s[:, r], s[:, u], s[:, c], z], 1).T)
        zb = jnp.zeros((256, 64), F32)
        wb[dy * 256 : (dy + 1) * 256, :] = jnp.concatenate([back[0], back[1], zb, back[2]], 1).astype(BF16)


def arrange_weights(iw, sw):
    return pl.pallas_call(
        weights_kernel,
        out_shape=(jax.ShapeDtypeStruct((1152, 256), BF16), jax.ShapeDtypeStruct((768, 256), BF16)),
        compiler_params=mosaic_params(16 * 2**20),
        name="arrange_weights",
    )(jnp.swapaxes(iw, 1, 2), jnp.swapaxes(sw, 1, 2))


def main_kernel(
    tr, tc, nrow, ncol, flat_rows,
    ea, eb, own, nb_core, far_1, far_2, wf, wb,
    final_ref, grad_ref, mine_ref, send_ref,
    x1, x2, f2, xd, p, o, ru1, t1, direct, mask, dw, tmp,
):
    pitch = tc + GAP
    ext = tr + 2 * HALO
    total = xd.shape[1]
    pad = 8
    row = lax.axis_index("row")
    col = lax.axis_index("col")
    parity = lax.rem(row, 2)
    lane_low = lax.broadcasted_iota(jnp.int32, (1, 128), 1) < 64

    z8 = jnp.zeros((8, 128), F32)
    for ref in (x1, f2, x2):
        ref[0 : pad + 8, :] = jnp.zeros((pad + 8, 128), F32)
        tail = ref.shape[0] - (pad + ext * pitch + 8)
        ref[pad + ext * pitch + 8 :, :] = jnp.zeros((tail, 128), F32)
    for r in (0, ext - 1):
        f2[pad + r * pitch + GAP : pad + (r + 1) * pitch, :] = jnp.zeros((tc, 128), F32)

    col_even = lax.rem(col, 2) == 0
    va, vb = ea[...].astype(F32), eb[...].astype(F32)
    lefts, rights = jnp.where(col_even, vb, va), jnp.where(col_even, va, vb)
    lo, hi = slice(0, 128), slice(128, 256)

    def place(ref, start, cells, count):
        for i in range(count):
            at = (start + i) * pitch + pad
            if not isinstance(start, int):
                at = pl.multiple_of(at, 8)
            ref[pl.ds(at + GAP, tc), :] = cells[i * tc : (i + 1) * tc]

    def place_edges(start, first, count):
        for i in range(count):
            at = (start + i) * pitch + pad
            if not isinstance(start, int):
                at = pl.multiple_of(at, 8)
            e = slice((first + i) * EDGE, (first + i + 1) * EDGE)
            for ref, lanes in ((x1, lo), (f2, hi)):
                ref[pl.ds(at + EDGE, EDGE), :] = lefts[e, lanes]
                ref[pl.ds(at + pitch, EDGE), :] = rights[e, lanes]

    near = (1 - parity) * (HALO + tr)
    far = parity * (HALO + tr)
    place(x1, HALO, own[:, lo].astype(F32), tr)
    place(f2, HALO, own[:, hi].astype(F32), tr)
    place_edges(HALO, 0, tr)
    place(x1, near, nb_core[:, lo].astype(F32), HALO)
    place(f2, near, nb_core[:, hi].astype(F32), HALO)
    place_edges(near, tr, HALO)
    place(x1, far, far_1[...].astype(F32), HALO)
    place(f2, far + 1 - parity, far_2[...].astype(F32), HALO - 1)
    place_edges(far, tr + HALO, HALO)

    mask[0:8, :] = z8
    tail = mask.shape[0] - (ext * pitch + 8)
    mask[ext * pitch + 8 :, :] = jnp.zeros((tail, 128), F32)
    has_left = (col > 0).astype(F32)
    has_right = (col < ncol - 1).astype(F32)
    for r in range(ext):
        if r < HALO:
            ok = (row > 0).astype(F32)
        elif r >= HALO + tr:
            ok = (row < nrow - 1).astype(F32)
        else:
            ok = jnp.float32(1.0)
        at = r * pitch
        mask[at + EDGE : at + GAP, :] = jnp.full((EDGE, 128), ok * has_left, F32)
        mask[at + GAP : at + pitch, :] = jnp.full((tc, 128), ok, F32)
        mask[at + pitch : at + pitch + EDGE, :] = jnp.full((EDGE, 128), ok * has_right, F32)

    def spread_columns(src, t):
        step = 288
        for n in range(0, total, step):
            m = min(step, total - n)
            for dx in range(3):
                xd[t, n : n + m, dx * 128 : (dx + 1) * 128] = src[
                    pad + n + dx - 1 : pad + n + dx - 1 + m, :
                ].astype(BF16)

    def gates(t, n, m):
        g = None
        for dy in range(3):
            at = n + (dy - 1) * pitch
            d = jnp.dot(
                xd[t, at : at + m, :],
                wf[dy * 384 : (dy + 1) * 384, :],
                preferred_element_type=F32,
            )
            g = d if g is None else g + d
        g1, g2 = g[:, :128], g[:, 128:]
        ru = 0.5 * jnp.tanh(0.5 * g1) + 0.5
        c = jnp.tanh(g2 + pltpu.roll(ru * g2, 64, 1))
        return ru, jnp.where(lane_low, g2, c)

    def pre_grads(g, s, ru, tt):
        om = 1.0 - ru
        pc = g * om * (1.0 - tt * tt)
        ph = pltpu.roll(pc, 64, 1) * ru
        pa = jnp.where(lane_low, ph * tt, g * (s - tt) * ru) * om
        pb = jnp.where(lane_low, ph, pc)
        return pa.astype(BF16), pb.astype(BF16)

    spread_columns(x1, 0)
    first = pitch
    m = 256
    count = -(-((ext - 2) * pitch + GAP) // m)
    for i in range(count):
        n = first + i * m
        ru, tt = gates(0, n, m)
        s = x1[pad + n : pad + n + m, :]
        new = (tt + ru * (s - tt)) * mask[n : n + m, :]
        new = new.astype(BF16).astype(F32)
        x2[pad + n : pad + n + m, :] = jnp.where(lane_low, f2[pad + n : pad + n + m, :], new)
        ru1[n : n + m, :] = ru
        t1[n : n + m, :] = tt
    done = first + count * m
    x2[pad + done :, :] = jnp.zeros((x2.shape[0] - pad - done, 128), F32)
    x2[pad + 8 : pad + first, :] = jnp.zeros((first - 8, 128), F32)

    spread_columns(x2, 1)
    first = 2 * pitch
    count = -(-((ext - 4) * pitch + GAP) // m)
    p[0:first, :] = jnp.zeros((first, 256), BF16)
    done = first + count * m
    p[done:, :] = jnp.zeros((p.shape[0] - done, 256), BF16)
    for i in range(count):
        n = first + i * m
        ru, tt = gates(1, n, m)
        s = x2[pad + n : pad + n + m, :]
        o[n : n + m, 0:128] = tt + ru * (s - tt)
        g = f2[pad + n : pad + n + m, :]
        pa, pb = pre_grads(g, s, ru, tt)
        p[n : n + m, 0:128] = pa
        p[n : n + m, 128:256] = pb
        direct[n : n + m, :] = g * ru
    ch = 64
    for r in range(tr):
        at = (HALO + r) * pitch + GAP
        tmp[pl.ds(r, ch, stride=tr), :] = o[at : at + tc, 0:128].T[64:, :]
    final_ref[...] = tmp[...].reshape(ch, tr, tc).astype(BF16)

    def weight_grads(t, add):
        pt = jnp.concatenate(
            [
                p[(HALO + r) * pitch + GAP : (HALO + r) * pitch + GAP + tc, :].T
                for r in range(tr)
            ],
            1,
        )
        for dy in range(3):
            at = [(HALO + r + dy - 1) * pitch + GAP for r in range(tr)]
            x = jnp.concatenate([xd[t, k : k + tc, :] for k in at], 0)
            d = jnp.dot(pt, x, preferred_element_type=F32)
            dw[dy] = dw[dy] + d if add else d

    def back_data(first, size, step):
        n = first
        while n < first + size:
            m = min(step, first + size - n)
            acc = None
            for dy in range(3):
                at = n - (dy - 1) * pitch
                d = jnp.dot(
                    p[at : at + m, :],
                    wb[dy * 256 : (dy + 1) * 256, :],
                    preferred_element_type=F32,
                )
                acc = d if acc is None else acc + d
            o[n : n + m, :] = acc
            n += m

    def gathered(n, m):
        return (
            pltpu.roll(o[n + 1 : n + 1 + m, 0:128], 64, 1)
            + o[n : n + m, 0:128]
            + o[n - 1 : n - 1 + m, 128:256]
        )

    weight_grads(1, False)
    back_data(3 * pitch - 16, (ext - 6) * pitch + 2 * GAP + 96, 256)

    first = 3 * pitch
    count = -(-((ext - 6) * pitch + GAP) // m)
    for i in range(count):
        n = first + i * m
        g = (direct[n : n + m, :] + gathered(n, m)) * mask[n : n + m, :]
        ru = ru1[n : n + m, :]
        pa, pb = pre_grads(g, x1[pad + n : pad + n + m, :], ru, t1[n : n + m, :])
        p[n : n + m, 0:128] = pa
        p[n : n + m, 128:256] = pb
        direct[n : n + m, :] = g * ru
    weight_grads(0, True)
    back_data(HALO * pitch, tr * pitch + GAP, 256)
    for r in range(tr):
        at = (HALO + r) * pitch + GAP
        g = direct[at : at + tc, :] + gathered(at, tc)
        grad_ref[pl.ds(r, ch, stride=tr), :] = g.T[64:, :]

    half = flat_rows // 2
    flat = o
    for tap in range(9):
        dy, dx = tap // 3, tap % 3
        d = dw[dy, :, dx * 128 : (dx + 1) * 128]
        at = tap * 192
        flat[at : at + 128, 0:128] = d[:128]
        flat[at + 128 : at + 192, 0:128] = jnp.where(lane_low, d[192:256], d[128:192])
    if flat_rows > 9 * 192:
        flat[9 * 192 : flat_rows, 0:128] = jnp.zeros((flat_rows - 9 * 192, 128), F32)
    chips = nrow // 2
    size = half // chips
    chip = lax.div(row, 2)
    for i in range(chips):
        part = jnp.bitwise_xor(chip, i) * size
        at = slice(i * size, (i + 1) * size)
        mine_ref[at, :] = flat[pl.ds(pl.multiple_of(parity * half + part, 16), size), 0:128]
        send_ref[at, :] = flat[
            pl.ds(pl.multiple_of((1 - parity) * half + part, 16), size), 0:128
        ].astype(BF16)


def main(ea, eb, own, nb_core, far_1, far_2, wf, wb, ch, tr, tc, flat_rows):
    nrow, ncol = lax.axis_size("row"), lax.axis_size("col")
    pitch = tc + GAP
    ext = tr + 2 * HALO
    cells = (ext + 1) * pitch + GAP
    cells = -(-cells // 16) * 16
    o_rows = max(cells, flat_rows)
    half = flat_rows // 2
    return pl.pallas_call(
        functools.partial(main_kernel, tr, tc, nrow, ncol, flat_rows),
        out_shape=(
            jax.ShapeDtypeStruct((ch, tr, tc), BF16),
            jax.ShapeDtypeStruct((ch * tr, tc), F32),
            jax.ShapeDtypeStruct((half, 128), F32),
            jax.ShapeDtypeStruct((half, 128), BF16),
        ),
        scratch_shapes=[
            pltpu.VMEM((cells + 16, 128), F32),
            pltpu.VMEM((cells + 16, 128), F32),
            pltpu.VMEM((cells + 16, 128), F32),
            pltpu.VMEM((2, cells, 384), BF16),
            pltpu.VMEM((cells, 256), BF16),
            pltpu.VMEM((o_rows, 256), F32),
            pltpu.VMEM((cells, 128), F32),
            pltpu.VMEM((cells, 128), F32),
            pltpu.VMEM((cells, 128), F32),
            pltpu.VMEM((cells, 128), F32),
            pltpu.VMEM((3, 256, 384), F32),
            pltpu.VMEM((ch * tr, tc), F32),
        ],
        compiler_params=mosaic_params(48 * 2**20),
        cost_estimate=pl.CostEstimate(flops=3000000000, bytes_accessed=4000000, transcendentals=600000),
        name="steps",
    )(ea, eb, own, nb_core, far_1, far_2, wf, wb)


def add_core_kernel(mine, got, first, *rest):
    size = first.shape[0]
    first[...] = mine[:size] + got[:size].astype(F32)
    for i, ref in enumerate(rest):
        at = slice((i + 1) * size, (i + 2) * size)
        ref[...] = (mine[at] + got[at].astype(F32)).astype(BF16)


def add_core(mine, got, chips):
    size = mine.shape[0] // chips
    part = jax.ShapeDtypeStruct((size, 128), BF16)
    return pl.pallas_call(
        add_core_kernel,
        out_shape=(jax.ShapeDtypeStruct((size, 128), F32),) + (part,) * (chips - 1),
        compiler_params=mosaic_params(16 * 2**20),
        name="add_core",
    )(mine, got)


def tree_sum_kernel(scale, *refs):
    values = [r[...].astype(F32) for r in refs[:-1]]
    while len(values) > 1:
        values = [values[i] + values[i + 1] for i in range(0, len(values), 2)]
    refs[-1][...] = (values[0] * scale).astype(BF16)


def tree_sum(parts, scale, name):
    return pl.pallas_call(
        functools.partial(tree_sum_kernel, scale),
        out_shape=jax.ShapeDtypeStruct(parts[0].shape, BF16),
        compiler_params=mosaic_params(16 * 2**20),
        name=name,
    )(*parts)


def join_kernel(*refs):
    size = refs[0].shape[0]
    for i, r in enumerate(refs[:-1]):
        refs[-1][i * size : (i + 1) * size, :] = r[...]


def join(parts):
    size = parts[0].shape[0]
    return pl.pallas_call(
        join_kernel,
        out_shape=jax.ShapeDtypeStruct((size * len(parts), 128), BF16),
        compiler_params=mosaic_params(16 * 2**20),
        name="join",
    )(*parts)


def unpack_kernel(chips, mine, other, gi, gs, flat):
    half = mine.shape[0]
    size = half // chips
    row = lax.axis_index("row")
    parity, chip = lax.rem(row, 2), lax.div(row, 2)
    for i in range(chips):
        part = jnp.bitwise_xor(chip, i) * size
        at = slice(i * size, (i + 1) * size)
        flat[pl.ds(pl.multiple_of(parity * half + part, 16), size), :] = mine[at].astype(F32)
        flat[pl.ds(pl.multiple_of((1 - parity) * half + part, 16), size), :] = other[at].astype(F32)
    for tap in range(9):
        at = tap * 192
        v = jnp.concatenate(
            [flat[at + 64 : at + 128, :], flat[at : at + 64, :], flat[at + 128 : at + 192, :]], 0
        ).T
        gi[tap] = v[:64]
        gs[tap] = v[64:]


def unpack(mine, other, chips, shape):
    shape = jax.ShapeDtypeStruct((shape[0], shape[2], shape[1]), F32)
    gi, gs = pl.pallas_call(
        functools.partial(unpack_kernel, chips),
        out_shape=(shape, shape),
        scratch_shapes=[pltpu.VMEM((2 * mine.shape[0], 128), F32)],
        compiler_params=mosaic_params(24 * 2**20),
        name="unpack",
    )(mine, other)
    return jnp.swapaxes(gi, 1, 2), jnp.swapaxes(gs, 1, 2)


def pairs(count, first):
    found = []
    for i in range(first, count - 1, 2):
        found += [(i, i + 1), (i + 1, i)]
    return found


def local(frames, state, input_weight, state_weight, cotangent):
    ch, tr, tc = state.shape
    nrow, ncol = lax.axis_size("row"), lax.axis_size("col")
    core_pairs = [(i, i ^ 1) for i in range(nrow)]
    far_pairs = pairs(nrow, 1)
    corners, to_core, to_far_1, to_far_2, own, left, right = pack(frames, state, cotangent)
    corners = lax.ppermute(corners, "row", far_pairs)
    nb_core = lax.ppermute(to_core, "row", core_pairs)
    far_1 = lax.ppermute(to_far_1, "row", far_pairs)
    far_2 = lax.ppermute(to_far_2, "row", far_pairs)
    wf, wb = arrange_weights(input_weight, state_weight)
    a, b = edges(corners, nb_core, left, right, tr, tc)
    a = lax.ppermute(a, "col", pairs(ncol, 0))
    b = lax.ppermute(b, "col", pairs(ncol, 1))

    chips = nrow // 2
    size = -(-9 * 192 // (nrow * 16)) * 16
    final, grad, mine, send = main(a, b, own, nb_core, far_1, far_2, wf, wb, ch, tr, tc, size * nrow)
    got = lax.ppermute(send, "row", core_pairs)
    first, *rest = add_core(mine, got, chips)
    parts = [
        lax.ppermute(v, "row", [(r, r ^ (2 * i)) for r in range(nrow)])
        for i, v in enumerate(rest, 1)
    ]
    mine = tree_sum([first] + parts, 1.0, "sum_chips")
    parts = [
        lax.ppermute(mine, "col", [(c, c ^ i) for c in range(ncol)]) for i in range(1, ncol)
    ]
    scale = float((tr * nrow * tc * ncol) ** (-0.5))
    mine = tree_sum([mine] + parts, scale, "sum_col")
    parts = [
        lax.ppermute(mine, "row", [(r, r ^ (2 * i)) for r in range(nrow)])
        for i in range(1, chips)
    ]
    whole = join([mine] + parts)
    other = lax.ppermute(whole, "row", core_pairs)
    gi, gs = unpack(whole, other, chips, input_weight.shape)
    return final, grad.reshape(ch, tr, tc), gi, gs


def solution(mesh):
    in_specs = (P(None, None, "row", "col"), P(None, "row", "col"), P(), P(), P(None, "row", "col"))
    out_specs = (P(None, "row", "col"), P(None, "row", "col"), P(), P())
    return jax.shard_map(local, mesh=mesh, in_specs=in_specs, out_specs=out_specs, check_vma=False)
```

```python
import functools

import jax
import jax.numpy as jnp
from jax import lax
from jax.experimental import pallas as pl
from jax.experimental.pallas import tpu as pltpu
from jax.sharding import PartitionSpec as P

F32 = jnp.float32
BF16 = jnp.bfloat16

HALO = 4
EDGE = 8
GAP = 2 * EDGE


def mosaic_params(limit):
    return pltpu.CompilerParams(vmem_limit_bytes=limit)


def pack_kernel(
    tr, tc, fields,
    corners, to_core, to_far_a, to_far_b, to_far_c, own, left, right,
    rows_f32,
):
    ch = fields.shape[0] // 4
    for f, i in enumerate((0, 2, 1, 3)):
        rows_f32[f] = fields[i * ch : (i + 1) * ch].astype(F32).reshape(ch * tr, tc)
    lefts, rights = [], []
    for r in range(tr):
        rows = [rows_f32[f, pl.ds(r, ch, stride=tr), :] for f in range(4)]
        a = jnp.concatenate(rows[:2], 0).T
        b = jnp.concatenate(rows[2:], 0).T
        ab = jnp.concatenate([a, b], 1)
        own[r * tc : (r + 1) * tc, :] = ab.astype(BF16)
        lefts.append(ab[:EDGE])
        rights.append(ab[tc - EDGE :])
    left[...] = jnp.concatenate(lefts, 0).astype(BF16)
    right[...] = jnp.concatenate(rights, 0).astype(BF16)
    parity = lax.rem(lax.axis_index("row"), 2)
    block = HALO * tc
    last = (tr - HALO) * tc
    near = pl.multiple_of((1 - parity) * last, 16)
    far = pl.multiple_of(parity * last, 16)
    to_core[...] = own[pl.ds(near, block), :]
    to_far_a[...] = own[pl.ds(far, block // 2), 0:128]
    to_far_b[...] = own[pl.ds(pl.multiple_of(far + block // 2, 16), block // 2), 0:128]
    to_far_c[...] = own[pl.ds(pl.multiple_of(far + parity * tc, 16), block - tc), 128:256]
    edge = pl.multiple_of(parity * (tr - HALO) * EDGE, 16)
    corners[0 : HALO * EDGE, :] = left[pl.ds(edge, HALO * EDGE), :]
    corners[HALO * EDGE :, :] = right[pl.ds(edge, HALO * EDGE), :]


def pack(frames, state, cot):
    ch, tr, tc = state.shape
    edge = jax.ShapeDtypeStruct((tr * EDGE, 4 * ch), BF16)
    return pl.pallas_call(
        functools.partial(pack_kernel, tr, tc),
        out_shape=(
            jax.ShapeDtypeStruct((2 * HALO * EDGE, 4 * ch), BF16),
            jax.ShapeDtypeStruct((HALO * tc, 4 * ch), BF16),
            jax.ShapeDtypeStruct((HALO // 2 * tc, 2 * ch), BF16),
            jax.ShapeDtypeStruct((HALO // 2 * tc, 2 * ch), BF16),
            jax.ShapeDtypeStruct(((HALO - 1) * tc, 2 * ch), BF16),
            jax.ShapeDtypeStruct((tr * tc, 4 * ch), BF16),
            edge,
            edge,
        ),
        scratch_shapes=[
            pltpu.VMEM((4, ch * tr, tc), F32),
        ],
        compiler_params=mosaic_params(24 * 2**20),
        name="pack",
    )(jnp.concatenate([frames.reshape(2 * ch, tr, tc), state, cot], 0))


def edges_kernel(tr, tc, nrow, corners, core, left, right, a, b):
    n = HALO * EDGE
    nb = core[...].astype(F32)
    row = lax.axis_index("row")
    has_far = jnp.logical_and(row > 0, row < nrow - 1)
    far = jnp.where(has_far, corners[...].astype(F32), 0.0)
    lefts = [nb[i * tc : i * tc + EDGE] for i in range(HALO)]
    rights = [nb[(i + 1) * tc - EDGE : (i + 1) * tc] for i in range(HALO)]
    lft = jnp.concatenate([left[...].astype(F32)] + lefts + [far[:n]], 0)
    rgt = jnp.concatenate([right[...].astype(F32)] + rights + [far[n:]], 0)
    even = lax.rem(lax.axis_index("col"), 2) == 0
    a[...] = jnp.where(even, rgt, lft).astype(BF16)
    b[...] = jnp.where(even, lft, rgt).astype(BF16)


def edges(corners, core, left, right, tr, tc):
    shape = jax.ShapeDtypeStruct(((tr + 2 * HALO) * EDGE, left.shape[1]), BF16)
    return pl.pallas_call(
        functools.partial(edges_kernel, tr, tc, lax.axis_size("row")),
        out_shape=(shape, shape),
        compiler_params=mosaic_params(16 * 2**20),
        name="edges",
    )(corners, core, left, right)


def weights_kernel(iw, sw, wf, wb):
    z = jnp.zeros((64, 64), F32)
    for tap in range(9):
        i, s = iw[tap].astype(F32), sw[tap].astype(F32)
        u, r, c = slice(0, 64), slice(64, 128), slice(128, 192)
        at = tap * 128
        wf[at : at + 64, :] = jnp.concatenate([i[:, r], i[:, u], z, i[:, c]], 1).astype(BF16)
        wf[at + 64 : at + 128, :] = jnp.concatenate([s[:, r], s[:, u], s[:, c], z], 1).astype(BF16)
    for dy in range(3):
        back = []
        for dx in range(3):
            s = sw[3 * dy + dx].astype(F32)
            back.append(jnp.concatenate([s[:, r], s[:, u], s[:, c], z], 1).T)
        zb = jnp.zeros((256, 64), F32)
        wb[dy * 256 : (dy + 1) * 256, :] = jnp.concatenate([back[0], back[1], zb, back[2]], 1).astype(BF16)


def arrange_weights(iw, sw):
    return pl.pallas_call(
        weights_kernel,
        out_shape=(jax.ShapeDtypeStruct((1152, 256), BF16), jax.ShapeDtypeStruct((768, 256), BF16)),
        compiler_params=mosaic_params(16 * 2**20),
        name="arrange_weights",
    )(jnp.swapaxes(iw, 1, 2), jnp.swapaxes(sw, 1, 2))


def main_kernel(
    tr, tc, nrow, ncol, flat_rows,
    ea, eb, own, nb_core, far_a, far_b, far_c, wf, wb,
    final_ref, grad_ref, mine_ref, send_ref,
    x1, x2, f2, xd, p, o, ru1, t1, direct, mask, dw, tmp,
):
    pitch = tc + GAP
    ext = tr + 2 * HALO
    total = xd.shape[1]
    pad = 8
    row = lax.axis_index("row")
    col = lax.axis_index("col")
    parity = lax.rem(row, 2)
    lane_low = lax.broadcasted_iota(jnp.int32, (1, 128), 1) < 64

    z8 = jnp.zeros((8, 128), F32)
    for ref in (x1, f2, x2):
        ref[0 : pad + 8, :] = jnp.zeros((pad + 8, 128), F32)
        tail = ref.shape[0] - (pad + ext * pitch + 8)
        ref[pad + ext * pitch + 8 :, :] = jnp.zeros((tail, 128), F32)
    for r in (0, ext - 1):
        f2[pad + r * pitch + GAP : pad + (r + 1) * pitch, :] = jnp.zeros((tc, 128), F32)

    col_even = lax.rem(col, 2) == 0
    inner = jnp.logical_and(col > 0, col < ncol - 1)
    va, vb = ea[...].astype(F32), jnp.where(inner, eb[...].astype(F32), 0.0)
    lefts, rights = jnp.where(col_even, vb, va), jnp.where(col_even, va, vb)
    lo, hi = slice(0, 128), slice(128, 256)

    def place(ref, start, cells, count):
        for i in range(count):
            at = (start + i) * pitch + pad
            if not isinstance(start, int):
                at = pl.multiple_of(at, 8)
            ref[pl.ds(at + GAP, tc), :] = cells[i * tc : (i + 1) * tc]

    def place_edges(start, first, count):
        for i in range(count):
            at = (start + i) * pitch + pad
            if not isinstance(start, int):
                at = pl.multiple_of(at, 8)
            e = slice((first + i) * EDGE, (first + i + 1) * EDGE)
            for ref, lanes in ((x1, lo), (f2, hi)):
                ref[pl.ds(at + EDGE, EDGE), :] = lefts[e, lanes]
                ref[pl.ds(at + pitch, EDGE), :] = rights[e, lanes]

    near = (1 - parity) * (HALO + tr)
    far = parity * (HALO + tr)
    place(x1, HALO, own[:, lo].astype(F32), tr)
    place(f2, HALO, own[:, hi].astype(F32), tr)
    place_edges(HALO, 0, tr)
    place(x1, near, nb_core[:, lo].astype(F32), HALO)
    place(f2, near, nb_core[:, hi].astype(F32), HALO)
    place_edges(near, tr, HALO)
    has_far = jnp.logical_and(row > 0, row < nrow - 1)
    place(x1, far, jnp.where(has_far, far_a[...].astype(F32), 0.0), HALO // 2)
    place(x1, far + HALO // 2, jnp.where(has_far, far_b[...].astype(F32), 0.0), HALO // 2)
    place(f2, far + 1 - parity, jnp.where(has_far, far_c[...].astype(F32), 0.0), HALO - 1)
    place_edges(far, tr + HALO, HALO)

    mask[0:8, :] = z8
    tail = mask.shape[0] - (ext * pitch + 8)
    mask[ext * pitch + 8 :, :] = jnp.zeros((tail, 128), F32)
    has_left = (col > 0).astype(F32)
    has_right = (col < ncol - 1).astype(F32)
    for r in range(ext):
        if r < HALO:
            ok = (row > 0).astype(F32)
        elif r >= HALO + tr:
            ok = (row < nrow - 1).astype(F32)
        else:
            ok = jnp.float32(1.0)
        at = r * pitch
        mask[at + EDGE : at + GAP, :] = jnp.full((EDGE, 128), ok * has_left, F32)
        mask[at + GAP : at + pitch, :] = jnp.full((tc, 128), ok, F32)
        mask[at + pitch : at + pitch + EDGE, :] = jnp.full((EDGE, 128), ok * has_right, F32)

    def spread_columns(src, t):
        step = 288
        for n in range(0, total, step):
            m = min(step, total - n)
            for dx in range(3):
                xd[t, n : n + m, dx * 128 : (dx + 1) * 128] = src[
                    pad + n + dx - 1 : pad + n + dx - 1 + m, :
                ].astype(BF16)

    def gates(t, n, m):
        g = None
        for dy in range(3):
            at = n + (dy - 1) * pitch
            d = jnp.dot(
                xd[t, at : at + m, :],
                wf[dy * 384 : (dy + 1) * 384, :],
                preferred_element_type=F32,
            )
            g = d if g is None else g + d
        g1, g2 = g[:, :128], g[:, 128:]
        ru = 0.5 * jnp.tanh(0.5 * g1) + 0.5
        c = jnp.tanh(g2 + pltpu.roll(ru * g2, 64, 1))
        return ru, jnp.where(lane_low, g2, c)

    def pre_grads(g, s, ru, tt):
        om = 1.0 - ru
        pc = g * om * (1.0 - tt * tt)
        ph = pltpu.roll(pc, 64, 1) * ru
        pa = jnp.where(lane_low, ph * tt, g * (s - tt) * ru) * om
        pb = jnp.where(lane_low, ph, pc)
        return pa.astype(BF16), pb.astype(BF16)

    spread_columns(x1, 0)
    first = pitch
    m = 256
    count = -(-((ext - 2) * pitch + GAP) // m)
    for i in range(count):
        n = first + i * m
        ru, tt = gates(0, n, m)
        s = x1[pad + n : pad + n + m, :]
        new = (tt + ru * (s - tt)) * mask[n : n + m, :]
        new = new.astype(BF16).astype(F32)
        x2[pad + n : pad + n + m, :] = jnp.where(lane_low, f2[pad + n : pad + n + m, :], new)
        ru1[n : n + m, :] = ru
        t1[n : n + m, :] = tt
    done = first + count * m
    x2[pad + done :, :] = jnp.zeros((x2.shape[0] - pad - done, 128), F32)
    x2[pad + 8 : pad + first, :] = jnp.zeros((first - 8, 128), F32)

    spread_columns(x2, 1)
    first = 2 * pitch
    count = -(-((ext - 4) * pitch + GAP) // m)
    p[0:first, :] = jnp.zeros((first, 256), BF16)
    done = first + count * m
    p[done:, :] = jnp.zeros((p.shape[0] - done, 256), BF16)
    for i in range(count):
        n = first + i * m
        ru, tt = gates(1, n, m)
        s = x2[pad + n : pad + n + m, :]
        o[n : n + m, 0:128] = tt + ru * (s - tt)
        g = f2[pad + n : pad + n + m, :]
        pa, pb = pre_grads(g, s, ru, tt)
        p[n : n + m, 0:128] = pa
        p[n : n + m, 128:256] = pb
        direct[n : n + m, :] = g * ru
    ch = 64
    for r in range(tr):
        at = (HALO + r) * pitch + GAP
        tmp[pl.ds(r, ch, stride=tr), :] = o[at : at + tc, 0:128].T[64:, :]
    final_ref[...] = tmp[...].reshape(ch, tr, tc).astype(BF16)

    def weight_grads(t, add):
        pt = jnp.concatenate(
            [
                p[(HALO + r) * pitch + GAP : (HALO + r) * pitch + GAP + tc, :].T
                for r in range(tr)
            ],
            1,
        )
        for dy in range(3):
            at = [(HALO + r + dy - 1) * pitch + GAP for r in range(tr)]
            x = jnp.concatenate([xd[t, k : k + tc, :] for k in at], 0)
            d = jnp.dot(pt, x, preferred_element_type=F32)
            dw[dy] = dw[dy] + d if add else d

    def back_data(first, size, step):
        n = first
        while n < first + size:
            m = min(step, first + size - n)
            acc = None
            for dy in range(3):
                at = n - (dy - 1) * pitch
                d = jnp.dot(
                    p[at : at + m, :],
                    wb[dy * 256 : (dy + 1) * 256, :],
                    preferred_element_type=F32,
                )
                acc = d if acc is None else acc + d
            o[n : n + m, :] = acc
            n += m

    def gathered(n, m):
        return (
            pltpu.roll(o[n + 1 : n + 1 + m, 0:128], 64, 1)
            + o[n : n + m, 0:128]
            + o[n - 1 : n - 1 + m, 128:256]
        )

    weight_grads(1, False)
    back_data(3 * pitch - 16, (ext - 6) * pitch + 2 * GAP + 96, 256)

    first = 3 * pitch
    count = -(-((ext - 6) * pitch + GAP) // m)
    for i in range(count):
        n = first + i * m
        g = (direct[n : n + m, :] + gathered(n, m)) * mask[n : n + m, :]
        ru = ru1[n : n + m, :]
        pa, pb = pre_grads(g, x1[pad + n : pad + n + m, :], ru, t1[n : n + m, :])
        p[n : n + m, 0:128] = pa
        p[n : n + m, 128:256] = pb
        direct[n : n + m, :] = g * ru
    weight_grads(0, True)
    back_data(HALO * pitch, tr * pitch + GAP, 256)
    for r in range(tr):
        at = (HALO + r) * pitch + GAP
        g = direct[at : at + tc, :] + gathered(at, tc)
        grad_ref[pl.ds(r, ch, stride=tr), :] = g.T[64:, :]

    half = flat_rows // 2
    flat = o
    for tap in range(9):
        dy, dx = tap // 3, tap % 3
        d = dw[dy, :, dx * 128 : (dx + 1) * 128]
        at = tap * 192
        flat[at : at + 128, 0:128] = d[:128]
        flat[at + 128 : at + 192, 0:128] = jnp.where(lane_low, d[192:256], d[128:192])
    if flat_rows > 9 * 192:
        flat[9 * 192 : flat_rows, 0:128] = jnp.zeros((flat_rows - 9 * 192, 128), F32)
    chips = nrow // 2
    size = half // chips
    chip = lax.div(row, 2)
    for i in range(chips):
        part = jnp.bitwise_xor(chip, i) * size
        at = slice(i * size, (i + 1) * size)
        mine_ref[at, :] = flat[pl.ds(pl.multiple_of(parity * half + part, 16), size), 0:128]
        send_ref[at, :] = flat[
            pl.ds(pl.multiple_of((1 - parity) * half + part, 16), size), 0:128
        ].astype(BF16)


def main(ea, eb, own, nb_core, far_a, far_b, far_c, wf, wb, ch, tr, tc, flat_rows):
    nrow, ncol = lax.axis_size("row"), lax.axis_size("col")
    pitch = tc + GAP
    ext = tr + 2 * HALO
    cells = (ext + 1) * pitch + GAP
    cells = -(-cells // 16) * 16
    o_rows = max(cells, flat_rows)
    half = flat_rows // 2
    return pl.pallas_call(
        functools.partial(main_kernel, tr, tc, nrow, ncol, flat_rows),
        out_shape=(
            jax.ShapeDtypeStruct((ch, tr, tc), BF16),
            jax.ShapeDtypeStruct((ch * tr, tc), F32),
            jax.ShapeDtypeStruct((half, 128), F32),
            jax.ShapeDtypeStruct((half, 128), BF16),
        ),
        scratch_shapes=[
            pltpu.VMEM((cells + 16, 128), F32),
            pltpu.VMEM((cells + 16, 128), F32),
            pltpu.VMEM((cells + 16, 128), F32),
            pltpu.VMEM((2, cells, 384), BF16),
            pltpu.VMEM((cells, 256), BF16),
            pltpu.VMEM((o_rows, 256), F32),
            pltpu.VMEM((cells, 128), F32),
            pltpu.VMEM((cells, 128), F32),
            pltpu.VMEM((cells, 128), F32),
            pltpu.VMEM((cells, 128), F32),
            pltpu.VMEM((3, 256, 384), F32),
            pltpu.VMEM((ch * tr, tc), F32),
        ],
        compiler_params=mosaic_params(48 * 2**20),
        cost_estimate=pl.CostEstimate(flops=3000000000, bytes_accessed=4000000, transcendentals=600000),
        name="steps",
    )(ea, eb, own, nb_core, far_a, far_b, far_c, wf, wb)


def add_core_kernel(mine, got, first, *rest):
    size = first.shape[0]
    first[...] = mine[:size] + got[:size].astype(F32)
    for i, ref in enumerate(rest):
        at = slice((i + 1) * size, (i + 2) * size)
        ref[...] = (mine[at] + got[at].astype(F32)).astype(BF16)


def add_core(mine, got, chips):
    size = mine.shape[0] // chips
    part = jax.ShapeDtypeStruct((size, 128), BF16)
    return pl.pallas_call(
        add_core_kernel,
        out_shape=(jax.ShapeDtypeStruct((size, 128), F32),) + (part,) * (chips - 1),
        compiler_params=mosaic_params(16 * 2**20),
        name="add_core",
    )(mine, got)


def tree_sum_kernel(scale, *refs):
    values = [r[...].astype(F32) for r in refs[:-1]]
    while len(values) > 1:
        values = [values[i] + values[i + 1] for i in range(0, len(values), 2)]
    refs[-1][...] = (values[0] * scale).astype(BF16)


def tree_sum(parts, scale, name):
    return pl.pallas_call(
        functools.partial(tree_sum_kernel, scale),
        out_shape=jax.ShapeDtypeStruct(parts[0].shape, BF16),
        compiler_params=mosaic_params(16 * 2**20),
        name=name,
    )(*parts)


def join_kernel(*refs):
    size = refs[0].shape[0]
    for i, r in enumerate(refs[:-1]):
        refs[-1][i * size : (i + 1) * size, :] = r[...]


def join(parts):
    size = parts[0].shape[0]
    return pl.pallas_call(
        join_kernel,
        out_shape=jax.ShapeDtypeStruct((size * len(parts), 128), BF16),
        compiler_params=mosaic_params(16 * 2**20),
        name="join",
    )(*parts)


def unpack_kernel(chips, mine, other, gi, gs, flat):
    half = mine.shape[0]
    size = half // chips
    row = lax.axis_index("row")
    parity, chip = lax.rem(row, 2), lax.div(row, 2)
    for i in range(chips):
        part = jnp.bitwise_xor(chip, i) * size
        at = slice(i * size, (i + 1) * size)
        flat[pl.ds(pl.multiple_of(parity * half + part, 16), size), :] = mine[at].astype(F32)
        flat[pl.ds(pl.multiple_of((1 - parity) * half + part, 16), size), :] = other[at].astype(F32)
    for tap in range(9):
        at = tap * 192
        v = jnp.concatenate(
            [flat[at + 64 : at + 128, :], flat[at : at + 64, :], flat[at + 128 : at + 192, :]], 0
        ).T
        gi[tap] = v[:64]
        gs[tap] = v[64:]


def unpack(mine, other, chips, shape):
    shape = jax.ShapeDtypeStruct((shape[0], shape[2], shape[1]), F32)
    gi, gs = pl.pallas_call(
        functools.partial(unpack_kernel, chips),
        out_shape=(shape, shape),
        scratch_shapes=[pltpu.VMEM((2 * mine.shape[0], 128), F32)],
        compiler_params=mosaic_params(24 * 2**20),
        name="unpack",
    )(mine, other)
    return jnp.swapaxes(gi, 1, 2), jnp.swapaxes(gs, 1, 2)


def swaps(nrow, ncol, partner):
    return [
        (r * ncol + c, partner(r, c)[0] * ncol + partner(r, c)[1])
        for r in range(nrow)
        for c in range(ncol)
    ]


def exchanges(nrow, ncol):
    def core(r, c):
        return r ^ 1, c

    def far(r, c):
        if r in (0, nrow - 1):
            return r, c ^ 1
        return r + 1 if r % 2 else r - 1, c

    def even_columns(r, c):
        return r, c ^ 1

    def odd_columns(r, c):
        if c in (0, ncol - 1):
            return r ^ 1, c
        return r, c + 1 if c % 2 else c - 1

    return [swaps(nrow, ncol, f) for f in (core, far, even_columns, odd_columns)]


def local(frames, state, input_weight, state_weight, cotangent):
    ch, tr, tc = state.shape
    nrow, ncol = lax.axis_size("row"), lax.axis_size("col")
    grid = ("row", "col")
    core_pairs, far_pairs, even_pairs, odd_pairs = exchanges(nrow, ncol)
    corners, to_core, *to_far, own, left, right = pack(frames, state, cotangent)
    corners = lax.ppermute(corners, grid, far_pairs)
    nb_core = lax.ppermute(to_core, grid, core_pairs)
    far_a, far_b, far_c = [lax.ppermute(v, grid, far_pairs) for v in to_far]
    wf, wb = arrange_weights(input_weight, state_weight)
    a, b = edges(corners, nb_core, left, right, tr, tc)
    a = lax.ppermute(a, grid, even_pairs)
    b = lax.ppermute(b, grid, odd_pairs)

    chips = nrow // 2
    size = -(-9 * 192 // (nrow * 16)) * 16
    final, grad, mine, send = main(a, b, own, nb_core, far_a, far_b, far_c, wf, wb, ch, tr, tc, size * nrow)
    got = lax.ppermute(send, grid, core_pairs)
    first, *rest = add_core(mine, got, chips)
    parts = [
        lax.ppermute(v, "row", [(r, r ^ (2 * i)) for r in range(nrow)])
        for i, v in enumerate(rest, 1)
    ]
    mine = tree_sum([first] + parts, 1.0, "sum_chips")
    parts = [
        lax.ppermute(mine, "col", [(c, c ^ i) for c in range(ncol)]) for i in range(1, ncol)
    ]
    scale = float((tr * nrow * tc * ncol) ** (-0.5))
    mine = tree_sum([mine] + parts, scale, "sum_col")
    parts = [
        lax.ppermute(mine, "row", [(r, r ^ (2 * i)) for r in range(nrow)])
        for i in range(1, chips)
    ]
    whole = join([mine] + parts)
    other = lax.ppermute(whole, grid, core_pairs)
    gi, gs = unpack(whole, other, chips, input_weight.shape)
    return final, grad.reshape(ch, tr, tc), gi, gs


def solution(mesh):
    in_specs = (P(None, None, "row", "col"), P(None, "row", "col"), P(), P(), P(None, "row", "col"))
    out_specs = (P(None, "row", "col"), P(None, "row", "col"), P(), P())
    return jax.shard_map(local, mesh=mesh, in_specs=in_specs, out_specs=out_specs, check_vma=False)
```

```python
import functools

import jax
import jax.numpy as jnp
from jax import lax
from jax.experimental import pallas as pl
from jax.experimental.pallas import tpu as pltpu
from jax.sharding import PartitionSpec as P

F32 = jnp.float32
BF16 = jnp.bfloat16

HALO = 4
EDGE = 4
GAP = 16


def mosaic_params(limit):
    return pltpu.CompilerParams(vmem_limit_bytes=limit)


def pack_kernel(
    tr, tc, fields,
    corners, to_core, to_far_a, to_far_b, to_far_c, own, left, right,
    rows_f32,
):
    ch = fields.shape[0] // 4
    for f, i in enumerate((0, 2, 1, 3)):
        rows_f32[f] = fields[i * ch : (i + 1) * ch].astype(F32).reshape(ch * tr, tc)
    lefts, rights = [], []
    for r in range(tr):
        rows = [rows_f32[f, pl.ds(r, ch, stride=tr), :] for f in range(4)]
        a = jnp.concatenate(rows[:2], 0).T
        b = jnp.concatenate(rows[2:], 0).T
        ab = jnp.concatenate([a, b], 1)
        own[r * tc : (r + 1) * tc, :] = ab.astype(BF16)
        lefts.append(ab[:EDGE])
        rights.append(ab[tc - EDGE :])
    left[...] = jnp.concatenate(lefts, 0).astype(BF16)
    right[...] = jnp.concatenate(rights, 0).astype(BF16)
    parity = lax.rem(lax.axis_index("row"), 2)
    block = HALO * tc
    last = (tr - HALO) * tc
    near = pl.multiple_of((1 - parity) * last, 16)
    far = pl.multiple_of(parity * last, 16)
    to_core[...] = own[pl.ds(near, block), :]
    to_far_a[...] = own[pl.ds(far, block // 2), 0:128]
    to_far_b[...] = own[pl.ds(pl.multiple_of(far + block // 2, 16), block // 2), 0:128]
    to_far_c[...] = own[pl.ds(pl.multiple_of(far + parity * 2 * tc, 16), 2 * tc), 128:256]
    edge = pl.multiple_of(parity * (tr - HALO) * EDGE, 16)
    n = HALO * EDGE
    corners[0:n, :] = left[pl.ds(edge, n), :]
    corners[n : 2 * n, :] = right[pl.ds(edge, n), :]
    third = own[pl.ds(pl.multiple_of(far + (2 - parity) * tc, 16), tc), 128:192].astype(F32)
    q = tc // 4
    corners[2 * n :, :] = jnp.concatenate(
        [third[i * q : (i + 1) * q] for i in range(4)], 1
    ).astype(BF16)


def pack(frames, state, cot):
    ch, tr, tc = state.shape
    edge = jax.ShapeDtypeStruct((tr * EDGE, 4 * ch), BF16)
    return pl.pallas_call(
        functools.partial(pack_kernel, tr, tc),
        out_shape=(
            jax.ShapeDtypeStruct((2 * HALO * EDGE + tc // 4, 4 * ch), BF16),
            jax.ShapeDtypeStruct((HALO * tc, 4 * ch), BF16),
            jax.ShapeDtypeStruct((HALO // 2 * tc, 2 * ch), BF16),
            jax.ShapeDtypeStruct((HALO // 2 * tc, 2 * ch), BF16),
            jax.ShapeDtypeStruct((HALO // 2 * tc, 2 * ch), BF16),
            jax.ShapeDtypeStruct((tr * tc, 4 * ch), BF16),
            edge,
            edge,
        ),
        scratch_shapes=[
            pltpu.VMEM((4, ch * tr, tc), F32),
        ],
        compiler_params=mosaic_params(24 * 2**20),
        name="pack",
    )(jnp.concatenate([frames.reshape(2 * ch, tr, tc), state, cot], 0))


def edges_kernel(tr, tc, nrow, corners, core, left, right, a, b):
    n = HALO * EDGE
    nb = core[...].astype(F32)
    row = lax.axis_index("row")
    has_far = jnp.logical_and(row > 0, row < nrow - 1)
    far = jnp.where(has_far, corners[...].astype(F32), 0.0)
    lefts = [nb[i * tc : i * tc + EDGE] for i in range(HALO)]
    rights = [nb[(i + 1) * tc - EDGE : (i + 1) * tc] for i in range(HALO)]
    lft = jnp.concatenate([left[...].astype(F32)] + lefts + [far[:n]], 0)
    rgt = jnp.concatenate([right[...].astype(F32)] + rights + [far[n : 2 * n]], 0)
    even = lax.rem(lax.axis_index("col"), 2) == 0
    a[...] = jnp.where(even, rgt, lft).astype(BF16)
    b[...] = jnp.where(even, lft, rgt).astype(BF16)


def edges(corners, core, left, right, tr, tc):
    shape = jax.ShapeDtypeStruct(((tr + 2 * HALO) * EDGE, left.shape[1]), BF16)
    return pl.pallas_call(
        functools.partial(edges_kernel, tr, tc, lax.axis_size("row")),
        out_shape=(shape, shape),
        compiler_params=mosaic_params(16 * 2**20),
        name="edges",
    )(corners, core, left, right)


def weights_kernel(iw, sw, wf, wb):
    z = jnp.zeros((64, 64), F32)
    for tap in range(9):
        i, s = iw[tap].astype(F32), sw[tap].astype(F32)
        u, r, c = slice(0, 64), slice(64, 128), slice(128, 192)
        at = tap * 128
        wf[at : at + 64, :] = jnp.concatenate([i[:, r], i[:, u], z, i[:, c]], 1).astype(BF16)
        wf[at + 64 : at + 128, :] = jnp.concatenate([s[:, r], s[:, u], s[:, c], z], 1).astype(BF16)
    for dy in range(3):
        back = []
        for dx in range(3):
            s = sw[3 * dy + dx].astype(F32)
            back.append(jnp.concatenate([s[:, r], s[:, u], s[:, c], z], 1).T)
        zb = jnp.zeros((256, 64), F32)
        wb[dy * 256 : (dy + 1) * 256, :] = jnp.concatenate([back[0], back[1], zb, back[2]], 1).astype(BF16)


def arrange_weights(iw, sw):
    return pl.pallas_call(
        weights_kernel,
        out_shape=(jax.ShapeDtypeStruct((1152, 256), BF16), jax.ShapeDtypeStruct((768, 256), BF16)),
        compiler_params=mosaic_params(16 * 2**20),
        name="arrange_weights",
    )(jnp.swapaxes(iw, 1, 2), jnp.swapaxes(sw, 1, 2))


def back_data(p, wb, o, pitch, first, size):
    n = first
    while n < first + size:
        m = min(256, first + size - n)
        x = jnp.concatenate([p[n - k * pitch : n - k * pitch + m, :] for k in (-1, 0, 1)], 1)
        o[n : n + m, :] = jnp.dot(x, wb[...], preferred_element_type=F32)
        n += m


def gathered(o, n, m):
    return (
        pltpu.roll(o[n + 1 : n + 1 + m, 0:128], 64, 1)
        + o[n : n + m, 0:128]
        + o[n - 1 : n - 1 + m, 128:256]
    )


def finish_kernel(tr, tc, p, direct, s2, wb, final_ref, grad_ref, token, o, tmp):
    pitch = tc + GAP
    ch = 64
    for r in range(tr):
        at = (HALO + r) * pitch + GAP
        tmp[pl.ds(r, ch, stride=tr), :] = s2[at : at + tc, :].T[64:, :]
    final_ref[...] = tmp[...].reshape(ch, tr, tc).astype(BF16)
    back_data(p, wb, o, pitch, HALO * pitch, tr * pitch + GAP)
    for r in range(tr):
        at = (HALO + r) * pitch + GAP
        g = direct[at : at + tc, :] + gathered(o, at, tc)
        grad_ref[pl.ds(r, ch, stride=tr), :] = g.T[64:, :]
    token[...] = jnp.zeros(token.shape, F32)


def finish(p, direct, s2, wb, ch, tr, tc):
    final, grad, token = pl.pallas_call(
        functools.partial(finish_kernel, tr, tc),
        out_shape=(
            jax.ShapeDtypeStruct((ch, tr, tc), BF16),
            jax.ShapeDtypeStruct((ch * tr, tc), F32),
            jax.ShapeDtypeStruct((8, 128), F32),
        ),
        scratch_shapes=[
            pltpu.VMEM((p.shape[0], 256), F32),
            pltpu.VMEM((ch * tr, tc), F32),
        ],
        compiler_params=mosaic_params(16 * 2**20),
        name="finish",
    )(p, direct, s2, wb)
    return final, grad.reshape(ch, tr, tc), token


def main_kernel(
    tr, tc, nrow, ncol, flat_rows,
    ea, eb, own, corners, nb_core, far_a, far_b, far_c, wf, wb,
    mine_ref, send_ref, p, direct, s2,
    x1, x2, f2, xd, o, ru1, t1, mask, dw,
):
    pitch = tc + GAP
    ext = tr + 2 * HALO
    total = xd.shape[1]
    pad = 8
    row = lax.axis_index("row")
    col = lax.axis_index("col")
    parity = lax.rem(row, 2)
    lane_low = lax.broadcasted_iota(jnp.int32, (1, 128), 1) < 64

    z8 = jnp.zeros((8, 128), F32)
    for ref in (x1, f2, x2):
        ref[0 : pad + 8, :] = jnp.zeros((pad + 8, 128), F32)
        tail = ref.shape[0] - (pad + ext * pitch + GAP)
        ref[pad + ext * pitch + GAP :, :] = jnp.zeros((tail, 128), F32)
    for r in (0, ext - 1):
        f2[pad + r * pitch + GAP : pad + (r + 1) * pitch, :] = jnp.zeros((tc, 128), F32)

    col_even = lax.rem(col, 2) == 0
    inner = jnp.logical_and(col > 0, col < ncol - 1)
    va, vb = ea[...].astype(F32), jnp.where(inner, eb[...].astype(F32), 0.0)
    lefts, rights = jnp.where(col_even, vb, va), jnp.where(col_even, va, vb)
    lo, hi = slice(0, 128), slice(128, 256)

    def place(ref, start, cells, count):
        for i in range(count):
            at = (start + i) * pitch + pad
            if not isinstance(start, int):
                at = pl.multiple_of(at, 8)
            ref[pl.ds(at + GAP, tc), :] = cells[i * tc : (i + 1) * tc]

    def in_order(v):
        own_rows, core_rows, far_rows = (
            v[: tr * EDGE], v[tr * EDGE : (tr + HALO) * EDGE], v[(tr + HALO) * EDGE :]
        )
        even = parity == 0
        above = jnp.where(even, far_rows, core_rows)
        below = jnp.where(even, core_rows, far_rows)
        return jnp.concatenate([above, own_rows, below], 0)

    lefts, rights = in_order(lefts), in_order(rights)
    none = jnp.zeros((EDGE, 256), F32)
    gap = jnp.zeros((GAP - 2 * EDGE, 256), F32)
    for r in range(ext + 1):
        rgt = rights[(r - 1) * EDGE : r * EDGE] if r > 0 else none
        lft = lefts[r * EDGE : (r + 1) * EDGE] if r < ext else none
        block = jnp.concatenate([rgt, gap, lft], 0)
        x1[pad + r * pitch : pad + r * pitch + GAP, :] = block[:, lo]
        f2[pad + r * pitch : pad + r * pitch + GAP, :] = block[:, hi]

    near = (1 - parity) * (HALO + tr)
    far = parity * (HALO + tr)
    place(x1, HALO, own[:, lo].astype(F32), tr)
    place(f2, HALO, own[:, hi].astype(F32), tr)
    place(x1, near, nb_core[:, lo].astype(F32), HALO)
    place(f2, near, nb_core[:, hi].astype(F32), HALO)
    has_far = jnp.logical_and(row > 0, row < nrow - 1)
    place(x1, far, jnp.where(has_far, far_a[...].astype(F32), 0.0), HALO // 2)
    place(x1, far + HALO // 2, jnp.where(has_far, far_b[...].astype(F32), 0.0), HALO // 2)
    place(f2, far + 2 * (1 - parity), jnp.where(has_far, far_c[...].astype(F32), 0.0), HALO // 2)
    third = jnp.where(has_far, corners[2 * HALO * EDGE :, :].astype(F32), 0.0)
    third = jnp.concatenate([third[:, i * 64 : (i + 1) * 64] for i in range(4)], 0)
    third = jnp.concatenate([third, jnp.zeros((tc, 64), F32)], 1)
    place(f2, far + 1 + parity, third, 1)

    mask[0:8, :] = z8
    tail = mask.shape[0] - (ext * pitch + 8)
    mask[ext * pitch + 8 :, :] = jnp.zeros((tail, 128), F32)
    has_left = (col > 0).astype(F32)
    has_right = (col < ncol - 1).astype(F32)
    for r in range(ext):
        if r < HALO:
            ok = (row > 0).astype(F32)
        elif r >= HALO + tr:
            ok = (row < nrow - 1).astype(F32)
        else:
            ok = jnp.float32(1.0)
        at = r * pitch
        mask[at + 8 : at + GAP, :] = jnp.full((8, 128), ok * has_left, F32)
        mask[at + GAP : at + pitch, :] = jnp.full((tc, 128), ok, F32)
        mask[at + pitch : at + pitch + 8, :] = jnp.full((8, 128), ok * has_right, F32)

    def spread_columns(src, t):
        step = 288
        for n in range(0, total, step):
            m = min(step, total - n)
            for dx in range(3):
                xd[t, n : n + m, dx * 128 : (dx + 1) * 128] = src[
                    pad + n + dx - 1 : pad + n + dx - 1 + m, :
                ].astype(BF16)

    def gates(t, n, m):
        x = jnp.concatenate([xd[t, n + k * pitch : n + k * pitch + m, :] for k in (-1, 0, 1)], 1)
        g = jnp.dot(x, wf[...], preferred_element_type=F32)
        g1, g2 = g[:, :128], g[:, 128:]
        ru = 0.5 * jnp.tanh(0.5 * g1) + 0.5
        c = jnp.tanh(g2 + pltpu.roll(ru * g2, 64, 1))
        return ru, jnp.where(lane_low, g2, c)

    def pre_grads(g, s, ru, tt):
        om = 1.0 - ru
        pc = g * om * (1.0 - tt * tt)
        ph = pltpu.roll(pc, 64, 1) * ru
        pa = jnp.where(lane_low, ph * tt, g * (s - tt) * ru) * om
        pb = jnp.where(lane_low, ph, pc)
        return pa.astype(BF16), pb.astype(BF16)

    spread_columns(x1, 0)
    first = pitch
    m = 256
    count = -(-((ext - 2) * pitch + GAP) // m)
    for i in range(count):
        n = first + i * m
        ru, tt = gates(0, n, m)
        s = x1[pad + n : pad + n + m, :]
        new = (tt + ru * (s - tt)) * mask[n : n + m, :]
        new = new.astype(BF16).astype(F32)
        x2[pad + n : pad + n + m, :] = jnp.where(lane_low, f2[pad + n : pad + n + m, :], new)
        ru1[n : n + m, :] = ru
        t1[n : n + m, :] = tt
    done = first + count * m
    x2[pad + done :, :] = jnp.zeros((x2.shape[0] - pad - done, 128), F32)
    x2[pad + 8 : pad + first, :] = jnp.zeros((first - 8, 128), F32)

    spread_columns(x2, 1)
    first = 2 * pitch
    count = -(-((ext - 4) * pitch + GAP) // m)
    p[0:first, :] = jnp.zeros((first, 256), BF16)
    done = first + count * m
    p[done:, :] = jnp.zeros((p.shape[0] - done, 256), BF16)
    for i in range(count):
        n = first + i * m
        ru, tt = gates(1, n, m)
        s = x2[pad + n : pad + n + m, :]
        s2[n : n + m, :] = tt + ru * (s - tt)
        g = f2[pad + n : pad + n + m, :]
        pa, pb = pre_grads(g, s, ru, tt)
        p[n : n + m, 0:128] = pa
        p[n : n + m, 128:256] = pb
        direct[n : n + m, :] = g * ru
    def weight_grads(t, add):
        pt = jnp.concatenate(
            [
                p[(HALO + r) * pitch + GAP : (HALO + r) * pitch + GAP + tc, :].T
                for r in range(tr)
            ],
            1,
        )
        x = jnp.concatenate(
            [
                jnp.concatenate(
                    [
                        xd[t, (HALO + r + k) * pitch + GAP : (HALO + r + k) * pitch + GAP + tc, :]
                        for k in (-1, 0, 1)
                    ],
                    1,
                )
                for r in range(tr)
            ],
            0,
        )
        d = jnp.dot(pt, x, preferred_element_type=F32)
        dw[...] = dw[...] + d if add else d

    weight_grads(1, False)
    back_data(p, wb, o, pitch, 3 * pitch - 16, (ext - 6) * pitch + 2 * GAP + 96)

    first = 3 * pitch
    count = -(-((ext - 6) * pitch + GAP) // m)
    for i in range(count):
        n = first + i * m
        g = (direct[n : n + m, :] + gathered(o, n, m)) * mask[n : n + m, :]
        ru = ru1[n : n + m, :]
        pa, pb = pre_grads(g, x1[pad + n : pad + n + m, :], ru, t1[n : n + m, :])
        p[n : n + m, 0:128] = pa
        p[n : n + m, 128:256] = pb
        direct[n : n + m, :] = g * ru
    weight_grads(0, True)
    half = flat_rows // 2
    flat = o
    for tap in range(9):
        d = dw[:, tap * 128 : (tap + 1) * 128]
        at = tap * 192
        flat[at : at + 128, 0:128] = d[:128]
        flat[at + 128 : at + 192, 0:128] = jnp.where(lane_low, d[192:256], d[128:192])
    if flat_rows > 9 * 192:
        flat[9 * 192 : flat_rows, 0:128] = jnp.zeros((flat_rows - 9 * 192, 128), F32)
    chips = nrow // 2
    size = half // chips
    chip = lax.div(row, 2)
    for i in range(chips):
        part = jnp.bitwise_xor(chip, i) * size
        at = slice(i * size, (i + 1) * size)
        mine_ref[at, :] = flat[pl.ds(pl.multiple_of(parity * half + part, 16), size), 0:128]
        send_ref[at, :] = flat[
            pl.ds(pl.multiple_of((1 - parity) * half + part, 16), size), 0:128
        ].astype(BF16)


def main(ea, eb, own, corners, nb_core, far_a, far_b, far_c, wf, wb, ch, tr, tc, flat_rows):
    nrow, ncol = lax.axis_size("row"), lax.axis_size("col")
    pitch = tc + GAP
    ext = tr + 2 * HALO
    cells = (ext + 1) * pitch + GAP
    cells = -(-cells // 16) * 16
    o_rows = max(cells, flat_rows)
    half = flat_rows // 2
    return pl.pallas_call(
        functools.partial(main_kernel, tr, tc, nrow, ncol, flat_rows),
        out_shape=(
            jax.ShapeDtypeStruct((half, 128), F32),
            jax.ShapeDtypeStruct((half, 128), BF16),
            jax.ShapeDtypeStruct((cells, 256), BF16),
            jax.ShapeDtypeStruct((cells, 128), F32),
            jax.ShapeDtypeStruct((cells, 128), F32),
        ),
        scratch_shapes=[
            pltpu.VMEM((cells + 16, 128), F32),
            pltpu.VMEM((cells + 16, 128), F32),
            pltpu.VMEM((cells + 16, 128), F32),
            pltpu.VMEM((2, cells, 384), BF16),
            pltpu.VMEM((o_rows, 256), F32),
            pltpu.VMEM((cells, 128), F32),
            pltpu.VMEM((cells, 128), F32),
            pltpu.VMEM((cells, 128), F32),
            pltpu.VMEM((256, 1152), F32),
        ],
        compiler_params=mosaic_params(32 * 2**20),
        cost_estimate=pl.CostEstimate(flops=3000000000, bytes_accessed=4000000, transcendentals=600000),
        name="steps",
    )(ea, eb, own, corners, nb_core, far_a, far_b, far_c, wf, wb)


def add_core_kernel(mine, got, first, *rest):
    size = first.shape[0]
    first[...] = mine[:size] + got[:size].astype(F32)
    for i, ref in enumerate(rest):
        at = slice((i + 1) * size, (i + 2) * size)
        ref[...] = (mine[at] + got[at].astype(F32)).astype(BF16)


def add_core(mine, got, chips):
    size = mine.shape[0] // chips
    part = jax.ShapeDtypeStruct((size, 128), BF16)
    return pl.pallas_call(
        add_core_kernel,
        out_shape=(jax.ShapeDtypeStruct((size, 128), F32),) + (part,) * (chips - 1),
        compiler_params=mosaic_params(16 * 2**20),
        name="add_core",
    )(mine, got)


def tree_sum_kernel(scale, count, *refs):
    values = [r[...].astype(F32) for r in refs[:count]]
    while len(values) > 1:
        values = [values[i] + values[i + 1] for i in range(0, len(values), 2)]
    refs[-1][...] = (values[0] * scale).astype(BF16)


def tree_sum(parts, scale, name, after=()):
    return pl.pallas_call(
        functools.partial(tree_sum_kernel, scale, len(parts)),
        out_shape=jax.ShapeDtypeStruct(parts[0].shape, BF16),
        compiler_params=mosaic_params(16 * 2**20),
        name=name,
    )(*parts, *after)


def join_kernel(*refs):
    size = refs[0].shape[0]
    for i, r in enumerate(refs[:-1]):
        refs[-1][i * size : (i + 1) * size, :] = r[...]


def join(parts):
    size = parts[0].shape[0]
    return pl.pallas_call(
        join_kernel,
        out_shape=jax.ShapeDtypeStruct((size * len(parts), 128), BF16),
        compiler_params=mosaic_params(16 * 2**20),
        name="join",
    )(*parts)


def put_parts(flat, parts, chips, chip):
    size = parts.shape[0] // chips
    for i in range(chips):
        at = pl.multiple_of(jnp.bitwise_xor(chip, i) * size, 16)
        flat[pl.ds(at, size), :] = parts[i * size : (i + 1) * size].astype(F32)


def put_taps(taps, gi, gs, stage, sems):
    copies = []
    for k, (tap, v) in enumerate(taps):
        stage[k] = jnp.concatenate([v[64:128], v[:64], v[128:]], 0).T
        for j, ref in enumerate((gi, gs)):
            copy = pltpu.make_async_copy(
                stage.at[k, pl.ds(j * 64, 64), :], ref.at[tap], sems.at[k, j]
            )
            copy.start()
            copies.append(copy)
    for copy in copies:
        copy.wait()


def whole_taps(flat, parity):
    gap = 5 * 192 - flat.shape[0]
    return [
        (parity * 5 + i, flat[pl.ds(pl.multiple_of(parity * gap + i * 192, 16), 192), :])
        for i in range(4)
    ]


def unpack_mine_kernel(chips, mine, gi, gs, flat, stage, sems):
    row = lax.axis_index("row")
    put_parts(flat, mine, chips, lax.div(row, 2))
    put_taps(whole_taps(flat, lax.rem(row, 2)), gi, gs, stage, sems)


def unpack_other_kernel(chips, mine, other, gi_in, gs_in, gi, gs, flat, flat_mine, stage, sems):
    del gi_in, gs_in
    row = lax.axis_index("row")
    parity = lax.rem(row, 2)
    put_parts(flat, other, chips, lax.div(row, 2))
    put_parts(flat_mine, mine, chips, lax.div(row, 2))
    taps = whole_taps(flat, 1 - parity)
    half = flat.shape[0]
    cut = half - 4 * 192
    even = parity == 0
    first = jnp.where(even, flat_mine[4 * 192 :, :], flat[4 * 192 :, :])
    second = jnp.where(even, flat[: 192 - cut, :], flat_mine[: 192 - cut, :])
    taps.append((4, jnp.concatenate([first, second], 0)))
    put_taps(taps, gi, gs, stage, sems)


def unpack(mine, other, chips, shape):
    half = mine.shape[0]
    shape = jax.ShapeDtypeStruct((shape[0], shape[2], shape[1]), F32)
    hbm, vmem = pl.BlockSpec(memory_space=pltpu.HBM), pl.BlockSpec(memory_space=pltpu.VMEM)
    flat = pltpu.VMEM((half, 128), F32)

    def stage(count):
        return [pltpu.VMEM((count, 128, 192), F32), pltpu.SemaphoreType.DMA((count, 2))]

    gi, gs = pl.pallas_call(
        functools.partial(unpack_mine_kernel, chips),
        out_shape=(shape, shape),
        out_specs=(hbm, hbm),
        scratch_shapes=[flat] + stage(4),
        compiler_params=mosaic_params(24 * 2**20),
        name="unpack_mine",
    )(mine)
    gi, gs = pl.pallas_call(
        functools.partial(unpack_other_kernel, chips),
        in_specs=[vmem, vmem, hbm, hbm],
        out_shape=(shape, shape),
        out_specs=(hbm, hbm),
        scratch_shapes=[flat, flat] + stage(5),
        input_output_aliases={2: 0, 3: 1},
        compiler_params=mosaic_params(24 * 2**20),
        name="unpack_other",
    )(mine, other, gi, gs)
    return jnp.swapaxes(gi, 1, 2), jnp.swapaxes(gs, 1, 2)


def swaps(nrow, ncol, partner):
    return [
        (r * ncol + c, partner(r, c)[0] * ncol + partner(r, c)[1])
        for r in range(nrow)
        for c in range(ncol)
    ]


def exchanges(nrow, ncol):
    def core(r, c):
        return r ^ 1, c

    def far(r, c):
        if r in (0, nrow - 1):
            return r, c ^ 1
        return r + 1 if r % 2 else r - 1, c

    def even_columns(r, c):
        return r, c ^ 1

    def odd_columns(r, c):
        if c in (0, ncol - 1):
            return r ^ 1, c
        return r, c + 1 if c % 2 else c - 1

    return [swaps(nrow, ncol, f) for f in (core, far, even_columns, odd_columns)]


def local(frames, state, input_weight, state_weight, cotangent):
    ch, tr, tc = state.shape
    nrow, ncol = lax.axis_size("row"), lax.axis_size("col")
    grid = ("row", "col")
    core_pairs, far_pairs, even_pairs, odd_pairs = exchanges(nrow, ncol)
    corners, to_core, *to_far, own, left, right = pack(frames, state, cotangent)
    corners = lax.ppermute(corners, grid, far_pairs)
    nb_core = lax.ppermute(to_core, grid, core_pairs)
    far_a, far_b, far_c = [lax.ppermute(v, grid, far_pairs) for v in to_far]
    wf, wb = arrange_weights(input_weight, state_weight)
    a, b = edges(corners, nb_core, left, right, tr, tc)
    a = lax.ppermute(a, grid, even_pairs)
    b = lax.ppermute(b, grid, odd_pairs)

    chips = nrow // 2
    size = -(-9 * 192 // (nrow * 16)) * 16
    mine, send, p, direct, s2 = main(a, b, own, corners, nb_core, far_a, far_b, far_c, wf, wb, ch, tr, tc, size * nrow)
    got = lax.ppermute(send, grid, core_pairs)
    final, grad, token = finish(p, direct, s2, wb, ch, tr, tc)
    first, *rest = add_core(mine, got, chips)
    parts = [
        lax.ppermute(v, "row", [(r, r ^ (2 * i)) for r in range(nrow)])
        for i, v in enumerate(rest, 1)
    ]
    mine = tree_sum([first] + parts, 1.0, "sum_chips", (token,))
    parts = [
        lax.ppermute(mine, "col", [(c, c ^ i) for c in range(ncol)]) for i in range(1, ncol)
    ]
    scale = float((tr * nrow * tc * ncol) ** (-0.5))
    mine = tree_sum([mine] + parts, scale, "sum_col")
    parts = [
        lax.ppermute(mine, "row", [(r, r ^ (2 * i)) for r in range(nrow)])
        for i in range(1, chips)
    ]
    whole = join([mine] + parts)
    other = lax.ppermute(whole, grid, core_pairs)
    gi, gs = unpack(whole, other, chips, input_weight.shape)
    return final, grad, gi, gs


def solution(mesh):
    in_specs = (P(None, None, "row", "col"), P(None, "row", "col"), P(), P(), P(None, "row", "col"))
    out_specs = (P(None, "row", "col"), P(None, "row", "col"), P(), P())
    return jax.shard_map(local, mesh=mesh, in_specs=in_specs, out_specs=out_specs, check_vma=False)
```

```python
import functools

import jax
import jax.numpy as jnp
from jax import lax
from jax.experimental import pallas as pl
from jax.experimental.pallas import tpu as pltpu
from jax.sharding import PartitionSpec as P

F32 = jnp.float32
BF16 = jnp.bfloat16

HALO = 4
EDGE = 4
GAP = 16


def mosaic_params(limit):
    return pltpu.CompilerParams(vmem_limit_bytes=limit)


def pack_kernel(
    tr, tc, fields,
    corners, to_core, to_far_a, to_far_b, to_far_c, own, left, right,
    rows_f32,
):
    ch = fields.shape[0] // 4
    for f, i in enumerate((0, 2, 1, 3)):
        rows_f32[f] = fields[i * ch : (i + 1) * ch].astype(F32).reshape(ch * tr, tc)
    lefts, rights = [], []
    for r in range(tr):
        rows = [rows_f32[f, pl.ds(r, ch, stride=tr), :] for f in range(4)]
        a = jnp.concatenate(rows[:2], 0).T
        b = jnp.concatenate(rows[2:], 0).T
        ab = jnp.concatenate([a, b], 1)
        own[r * tc : (r + 1) * tc, :] = ab.astype(BF16)
        lefts.append(ab[:EDGE])
        rights.append(ab[tc - EDGE :])
    left[...] = jnp.concatenate(lefts, 0).astype(BF16)
    right[...] = jnp.concatenate(rights, 0).astype(BF16)
    parity = lax.rem(lax.axis_index("row"), 2)
    block = HALO * tc
    last = (tr - HALO) * tc
    near = pl.multiple_of((1 - parity) * last, 16)
    far = pl.multiple_of(parity * last, 16)
    to_core[...] = own[pl.ds(near, block), :]
    to_far_a[...] = own[pl.ds(far, block // 2), 0:128]
    to_far_b[...] = own[pl.ds(pl.multiple_of(far + block // 2, 16), block // 2), 0:128]
    to_far_c[...] = own[pl.ds(pl.multiple_of(far + parity * 2 * tc, 16), 2 * tc), 128:256]
    edge = pl.multiple_of(parity * (tr - HALO) * EDGE, 16)
    n = HALO * EDGE
    corners[0:n, :] = left[pl.ds(edge, n), :]
    corners[n : 2 * n, :] = right[pl.ds(edge, n), :]
    third = own[pl.ds(pl.multiple_of(far + (2 - parity) * tc, 16), tc), 128:192].astype(F32)
    q = tc // 4
    corners[2 * n :, :] = jnp.concatenate(
        [third[i * q : (i + 1) * q] for i in range(4)], 1
    ).astype(BF16)


def pack(frames, state, cot):
    ch, tr, tc = state.shape
    edge = jax.ShapeDtypeStruct((tr * EDGE, 4 * ch), BF16)
    return pl.pallas_call(
        functools.partial(pack_kernel, tr, tc),
        out_shape=(
            jax.ShapeDtypeStruct((2 * HALO * EDGE + tc // 4, 4 * ch), BF16),
            jax.ShapeDtypeStruct((HALO * tc, 4 * ch), BF16),
            jax.ShapeDtypeStruct((HALO // 2 * tc, 2 * ch), BF16),
            jax.ShapeDtypeStruct((HALO // 2 * tc, 2 * ch), BF16),
            jax.ShapeDtypeStruct((HALO // 2 * tc, 2 * ch), BF16),
            jax.ShapeDtypeStruct((tr * tc, 4 * ch), BF16),
            edge,
            edge,
        ),
        scratch_shapes=[
            pltpu.VMEM((4, ch * tr, tc), F32),
        ],
        compiler_params=mosaic_params(24 * 2**20),
        name="pack",
    )(jnp.concatenate([frames.reshape(2 * ch, tr, tc), state, cot], 0))


def edges_kernel(tr, tc, nrow, corners, core, left, right, a, b):
    n = HALO * EDGE
    nb = core[...].astype(F32)
    row = lax.axis_index("row")
    has_far = jnp.logical_and(row > 0, row < nrow - 1)
    far = jnp.where(has_far, corners[...].astype(F32), 0.0)
    lefts = [nb[i * tc : i * tc + EDGE] for i in range(HALO)]
    rights = [nb[(i + 1) * tc - EDGE : (i + 1) * tc] for i in range(HALO)]
    lft = jnp.concatenate([left[...].astype(F32)] + lefts + [far[:n]], 0)
    rgt = jnp.concatenate([right[...].astype(F32)] + rights + [far[n : 2 * n]], 0)
    even = lax.rem(lax.axis_index("col"), 2) == 0
    a[...] = jnp.where(even, rgt, lft).astype(BF16)
    b[...] = jnp.where(even, lft, rgt).astype(BF16)


def edges(corners, core, left, right, tr, tc):
    shape = jax.ShapeDtypeStruct(((tr + 2 * HALO) * EDGE, left.shape[1]), BF16)
    return pl.pallas_call(
        functools.partial(edges_kernel, tr, tc, lax.axis_size("row")),
        out_shape=(shape, shape),
        compiler_params=mosaic_params(16 * 2**20),
        name="edges",
    )(corners, core, left, right)


def weights_kernel(iw, sw, wf, wb):
    z = jnp.zeros((64, 64), F32)
    for tap in range(9):
        i, s = iw[tap].astype(F32), sw[tap].astype(F32)
        u, r, c = slice(0, 64), slice(64, 128), slice(128, 192)
        at = tap * 128
        wf[at : at + 64, :] = jnp.concatenate([i[:, r], i[:, u], z, i[:, c]], 1).astype(BF16)
        wf[at + 64 : at + 128, :] = jnp.concatenate([s[:, r], s[:, u], s[:, c], z], 1).astype(BF16)
    for dy in range(3):
        back = []
        for dx in range(3):
            s = sw[3 * dy + dx].astype(F32)
            back.append(jnp.concatenate([s[:, r], s[:, u], s[:, c], z], 1).T)
        zb = jnp.zeros((256, 64), F32)
        wb[dy * 256 : (dy + 1) * 256, :] = jnp.concatenate([back[0], back[1], zb, back[2]], 1).astype(BF16)


def arrange_weights(iw, sw):
    return pl.pallas_call(
        weights_kernel,
        out_shape=(jax.ShapeDtypeStruct((1152, 256), BF16), jax.ShapeDtypeStruct((768, 256), BF16)),
        compiler_params=mosaic_params(16 * 2**20),
        name="arrange_weights",
    )(jnp.swapaxes(iw, 1, 2), jnp.swapaxes(sw, 1, 2))


def back_data(p, wb, o, pitch, first, size):
    n = first
    while n < first + size:
        m = min(256, first + size - n)
        x = jnp.concatenate([p[n - k * pitch : n - k * pitch + m, :] for k in (-1, 0, 1)], 1)
        o[n : n + m, :] = jnp.dot(x, wb[...], preferred_element_type=F32)
        n += m


def gathered(o, n, m):
    return (
        pltpu.roll(o[n + 1 : n + 1 + m, 0:128], 64, 1)
        + o[n : n + m, 0:128]
        + o[n - 1 : n - 1 + m, 128:256]
    )


def finish_kernel(tr, tc, p, direct, s2, wb, final_ref, grad_ref, token, o, tmp):
    pitch = tc + GAP
    ch = 64
    for r in range(tr):
        at = (HALO + r) * pitch + GAP
        tmp[pl.ds(r, ch, stride=tr), :] = s2[at : at + tc, :].T[64:, :]
    final_ref[...] = tmp[...].reshape(ch, tr, tc).astype(BF16)
    back_data(p, wb, o, pitch, HALO * pitch, tr * pitch + GAP)
    for r in range(tr):
        at = (HALO + r) * pitch + GAP
        g = direct[at : at + tc, :] + gathered(o, at, tc)
        grad_ref[pl.ds(r, ch, stride=tr), :] = g.T[64:, :]
    token[...] = jnp.zeros(token.shape, F32)


def finish(p, direct, s2, wb, ch, tr, tc):
    final, grad, token = pl.pallas_call(
        functools.partial(finish_kernel, tr, tc),
        out_shape=(
            jax.ShapeDtypeStruct((ch, tr, tc), BF16),
            jax.ShapeDtypeStruct((ch * tr, tc), F32),
            jax.ShapeDtypeStruct((8, 128), F32),
        ),
        scratch_shapes=[
            pltpu.VMEM((p.shape[0], 256), F32),
            pltpu.VMEM((ch * tr, tc), F32),
        ],
        compiler_params=mosaic_params(16 * 2**20),
        name="finish",
    )(p, direct, s2, wb)
    return final, grad.reshape(ch, tr, tc), token


def main_kernel(
    tr, tc, nrow, ncol, flat_rows,
    ea, eb, own, corners, nb_core, far_a, far_b, far_c, wf, wb,
    mine_ref, send_ref, p, direct, s2,
    x1, x2, f2, xd, o, ru1, t1, mask, dw,
):
    pitch = tc + GAP
    ext = tr + 2 * HALO
    total = xd.shape[1]
    pad = 8
    row = lax.axis_index("row")
    col = lax.axis_index("col")
    parity = lax.rem(row, 2)
    lane_low = lax.broadcasted_iota(jnp.int32, (1, 128), 1) < 64

    z8 = jnp.zeros((8, 128), F32)
    for ref in (x1, f2, x2):
        ref[0 : pad + 8, :] = jnp.zeros((pad + 8, 128), F32)
        tail = ref.shape[0] - (pad + ext * pitch + GAP)
        ref[pad + ext * pitch + GAP :, :] = jnp.zeros((tail, 128), F32)
    for r in (0, ext - 1):
        f2[pad + r * pitch + GAP : pad + (r + 1) * pitch, :] = jnp.zeros((tc, 128), F32)

    col_even = lax.rem(col, 2) == 0
    inner = jnp.logical_and(col > 0, col < ncol - 1)
    va, vb = ea[...].astype(F32), jnp.where(inner, eb[...].astype(F32), 0.0)
    lefts, rights = jnp.where(col_even, vb, va), jnp.where(col_even, va, vb)
    lo, hi = slice(0, 128), slice(128, 256)

    def place(ref, start, cells, count):
        for i in range(count):
            at = (start + i) * pitch + pad
            if not isinstance(start, int):
                at = pl.multiple_of(at, 8)
            ref[pl.ds(at + GAP, tc), :] = cells[i * tc : (i + 1) * tc]

    def in_order(v):
        own_rows, core_rows, far_rows = (
            v[: tr * EDGE], v[tr * EDGE : (tr + HALO) * EDGE], v[(tr + HALO) * EDGE :]
        )
        even = parity == 0
        above = jnp.where(even, far_rows, core_rows)
        below = jnp.where(even, core_rows, far_rows)
        return jnp.concatenate([above, own_rows, below], 0)

    lefts, rights = in_order(lefts), in_order(rights)
    none = jnp.zeros((EDGE, 256), F32)
    gap = jnp.zeros((GAP - 2 * EDGE, 256), F32)
    for r in range(ext + 1):
        rgt = rights[(r - 1) * EDGE : r * EDGE] if r > 0 else none
        lft = lefts[r * EDGE : (r + 1) * EDGE] if r < ext else none
        block = jnp.concatenate([rgt, gap, lft], 0)
        x1[pad + r * pitch : pad + r * pitch + GAP, :] = block[:, lo]
        f2[pad + r * pitch : pad + r * pitch + GAP, :] = block[:, hi]

    near = (1 - parity) * (HALO + tr)
    far = parity * (HALO + tr)
    place(x1, HALO, own[:, lo].astype(F32), tr)
    place(f2, HALO, own[:, hi].astype(F32), tr)
    place(x1, near, nb_core[:, lo].astype(F32), HALO)
    place(f2, near, nb_core[:, hi].astype(F32), HALO)
    has_far = jnp.logical_and(row > 0, row < nrow - 1)
    place(x1, far, jnp.where(has_far, far_a[...].astype(F32), 0.0), HALO // 2)
    place(x1, far + HALO // 2, jnp.where(has_far, far_b[...].astype(F32), 0.0), HALO // 2)
    place(f2, far + 2 * (1 - parity), jnp.where(has_far, far_c[...].astype(F32), 0.0), HALO // 2)
    third = jnp.where(has_far, corners[2 * HALO * EDGE :, :].astype(F32), 0.0)
    third = jnp.concatenate([third[:, i * 64 : (i + 1) * 64] for i in range(4)], 0)
    third = jnp.concatenate([third, jnp.zeros((tc, 64), F32)], 1)
    place(f2, far + 1 + parity, third, 1)

    mask[0:8, :] = z8
    tail = mask.shape[0] - (ext * pitch + 8)
    mask[ext * pitch + 8 :, :] = jnp.zeros((tail, 128), F32)
    has_left = (col > 0).astype(F32)
    has_right = (col < ncol - 1).astype(F32)
    for r in range(ext):
        if r < HALO:
            ok = (row > 0).astype(F32)
        elif r >= HALO + tr:
            ok = (row < nrow - 1).astype(F32)
        else:
            ok = jnp.float32(1.0)
        at = r * pitch
        mask[at + 8 : at + GAP, :] = jnp.full((8, 128), ok * has_left, F32)
        mask[at + GAP : at + pitch, :] = jnp.full((tc, 128), ok, F32)
        mask[at + pitch : at + pitch + 8, :] = jnp.full((8, 128), ok * has_right, F32)

    def spread_columns(src, t):
        step = 288
        for n in range(0, total, step):
            m = min(step, total - n)
            for dx in range(3):
                xd[t, n : n + m, dx * 128 : (dx + 1) * 128] = src[
                    pad + n + dx - 1 : pad + n + dx - 1 + m, :
                ].astype(BF16)

    def gates(t, n, m):
        x = jnp.concatenate([xd[t, n + k * pitch : n + k * pitch + m, :] for k in (-1, 0, 1)], 1)
        g = jnp.dot(x, wf[...], preferred_element_type=F32)
        g1, g2 = g[:, :128], g[:, 128:]
        ru = 0.5 * jnp.tanh(0.5 * g1) + 0.5
        c = jnp.tanh(g2 + pltpu.roll(ru * g2, 64, 1))
        return ru, jnp.where(lane_low, g2, c)

    def pre_grads(g, s, ru, tt):
        om = 1.0 - ru
        pc = g * om * (1.0 - tt * tt)
        ph = pltpu.roll(pc, 64, 1) * ru
        pa = jnp.where(lane_low, ph * tt, g * (s - tt) * ru) * om
        pb = jnp.where(lane_low, ph, pc)
        return pa.astype(BF16), pb.astype(BF16)

    spread_columns(x1, 0)
    first = pitch
    m = 128
    count = -(-((ext - 2) * pitch + GAP) // m)
    for i in range(count):
        n = first + i * m
        ru, tt = gates(0, n, m)
        s = x1[pad + n : pad + n + m, :]
        new = (tt + ru * (s - tt)) * mask[n : n + m, :]
        new = new.astype(BF16).astype(F32)
        x2[pad + n : pad + n + m, :] = jnp.where(lane_low, f2[pad + n : pad + n + m, :], new)
        ru1[n : n + m, :] = ru
        t1[n : n + m, :] = tt
    done = first + count * m
    x2[pad + done :, :] = jnp.zeros((x2.shape[0] - pad - done, 128), F32)
    x2[pad + 8 : pad + first, :] = jnp.zeros((first - 8, 128), F32)

    spread_columns(x2, 1)
    first = 2 * pitch
    count = -(-((ext - 4) * pitch + GAP) // m)
    p[0:first, :] = jnp.zeros((first, 256), BF16)
    done = first + count * m
    p[done:, :] = jnp.zeros((p.shape[0] - done, 256), BF16)
    for i in range(count):
        n = first + i * m
        ru, tt = gates(1, n, m)
        s = x2[pad + n : pad + n + m, :]
        s2[n : n + m, :] = tt + ru * (s - tt)
        g = f2[pad + n : pad + n + m, :]
        pa, pb = pre_grads(g, s, ru, tt)
        p[n : n + m, 0:128] = pa
        p[n : n + m, 128:256] = pb
        direct[n : n + m, :] = g * ru
    def weight_grads(t, add):
        pt = jnp.concatenate(
            [
                p[(HALO + r) * pitch + GAP : (HALO + r) * pitch + GAP + tc, :].T
                for r in range(tr)
            ],
            1,
        )
        x = jnp.concatenate(
            [
                jnp.concatenate(
                    [
                        xd[t, (HALO + r + k) * pitch + GAP : (HALO + r + k) * pitch + GAP + tc, :]
                        for k in (-1, 0, 1)
                    ],
                    1,
                )
                for r in range(tr)
            ],
            0,
        )
        d = jnp.dot(pt, x, preferred_element_type=F32)
        dw[...] = dw[...] + d if add else d

    weight_grads(1, False)
    back_data(p, wb, o, pitch, 3 * pitch - 16, (ext - 6) * pitch + 2 * GAP + 96)

    first = 3 * pitch
    count = -(-((ext - 6) * pitch + GAP) // m)
    for i in range(count):
        n = first + i * m
        g = (direct[n : n + m, :] + gathered(o, n, m)) * mask[n : n + m, :]
        ru = ru1[n : n + m, :]
        pa, pb = pre_grads(g, x1[pad + n : pad + n + m, :], ru, t1[n : n + m, :])
        p[n : n + m, 0:128] = pa
        p[n : n + m, 128:256] = pb
        direct[n : n + m, :] = g * ru
    weight_grads(0, True)
    half = flat_rows // 2
    flat = o
    for tap in range(9):
        d = dw[:, tap * 128 : (tap + 1) * 128]
        at = tap * 192
        flat[at : at + 128, 0:128] = d[:128]
        flat[at + 128 : at + 192, 0:128] = jnp.where(lane_low, d[192:256], d[128:192])
    if flat_rows > 9 * 192:
        flat[9 * 192 : flat_rows, 0:128] = jnp.zeros((flat_rows - 9 * 192, 128), F32)
    chips = nrow // 2
    size = half // chips
    chip = lax.div(row, 2)
    for i in range(chips):
        part = jnp.bitwise_xor(chip, i) * size
        at = slice(i * size, (i + 1) * size)
        mine_ref[at, :] = flat[pl.ds(pl.multiple_of(parity * half + part, 16), size), 0:128]
        send_ref[at, :] = flat[
            pl.ds(pl.multiple_of((1 - parity) * half + part, 16), size), 0:128
        ].astype(BF16)


def main(ea, eb, own, corners, nb_core, far_a, far_b, far_c, wf, wb, ch, tr, tc, flat_rows):
    nrow, ncol = lax.axis_size("row"), lax.axis_size("col")
    pitch = tc + GAP
    ext = tr + 2 * HALO
    cells = (ext + 1) * pitch + GAP
    cells = -(-cells // 16) * 16
    o_rows = max(cells, flat_rows)
    half = flat_rows // 2
    return pl.pallas_call(
        functools.partial(main_kernel, tr, tc, nrow, ncol, flat_rows),
        out_shape=(
            jax.ShapeDtypeStruct((half, 128), F32),
            jax.ShapeDtypeStruct((half, 128), BF16),
            jax.ShapeDtypeStruct((cells, 256), BF16),
            jax.ShapeDtypeStruct((cells, 128), F32),
            jax.ShapeDtypeStruct((cells, 128), F32),
        ),
        scratch_shapes=[
            pltpu.VMEM((cells + 16, 128), F32),
            pltpu.VMEM((cells + 16, 128), F32),
            pltpu.VMEM((cells + 16, 128), F32),
            pltpu.VMEM((2, cells, 384), BF16),
            pltpu.VMEM((o_rows, 256), F32),
            pltpu.VMEM((cells, 128), F32),
            pltpu.VMEM((cells, 128), F32),
            pltpu.VMEM((cells, 128), F32),
            pltpu.VMEM((256, 1152), F32),
        ],
        compiler_params=mosaic_params(32 * 2**20),
        cost_estimate=pl.CostEstimate(flops=3000000000, bytes_accessed=4000000, transcendentals=600000),
        name="steps",
    )(ea, eb, own, corners, nb_core, far_a, far_b, far_c, wf, wb)


def add_core_kernel(mine, got, first, *rest):
    size = first.shape[0]
    first[...] = mine[:size] + got[:size].astype(F32)
    for i, ref in enumerate(rest):
        at = slice((i + 1) * size, (i + 2) * size)
        ref[...] = (mine[at] + got[at].astype(F32)).astype(BF16)


def add_core(mine, got, chips):
    size = mine.shape[0] // chips
    part = jax.ShapeDtypeStruct((size, 128), BF16)
    return pl.pallas_call(
        add_core_kernel,
        out_shape=(jax.ShapeDtypeStruct((size, 128), F32),) + (part,) * (chips - 1),
        compiler_params=mosaic_params(16 * 2**20),
        name="add_core",
    )(mine, got)


def tree_sum_kernel(scale, count, *refs):
    values = [r[...].astype(F32) for r in refs[:count]]
    while len(values) > 1:
        values = [values[i] + values[i + 1] for i in range(0, len(values), 2)]
    refs[-1][...] = (values[0] * scale).astype(BF16)


def tree_sum(parts, scale, name, after=()):
    return pl.pallas_call(
        functools.partial(tree_sum_kernel, scale, len(parts)),
        out_shape=jax.ShapeDtypeStruct(parts[0].shape, BF16),
        compiler_params=mosaic_params(16 * 2**20),
        name=name,
    )(*parts, *after)


def join_kernel(*refs):
    size = refs[0].shape[0]
    for i, r in enumerate(refs[:-1]):
        refs[-1][i * size : (i + 1) * size, :] = r[...]


def join(parts):
    size = parts[0].shape[0]
    return pl.pallas_call(
        join_kernel,
        out_shape=jax.ShapeDtypeStruct((size * len(parts), 128), BF16),
        compiler_params=mosaic_params(16 * 2**20),
        name="join",
    )(*parts)


def put_parts(flat, parts, chips, chip):
    size = parts.shape[0] // chips
    for i in range(chips):
        at = pl.multiple_of(jnp.bitwise_xor(chip, i) * size, 16)
        flat[pl.ds(at, size), :] = parts[i * size : (i + 1) * size].astype(F32)


def put_taps(taps, gi, gs, stage, sems):
    copies = []
    for k, (tap, v) in enumerate(taps):
        stage[k] = jnp.concatenate([v[64:128], v[:64], v[128:]], 0).T
        for j, ref in enumerate((gi, gs)):
            copy = pltpu.make_async_copy(
                stage.at[k, pl.ds(j * 64, 64), :], ref.at[tap], sems.at[k, j]
            )
            copy.start()
            copies.append(copy)
    for copy in copies:
        copy.wait()


def whole_taps(flat, parity):
    gap = 5 * 192 - flat.shape[0]
    return [
        (parity * 5 + i, flat[pl.ds(pl.multiple_of(parity * gap + i * 192, 16), 192), :])
        for i in range(4)
    ]


def unpack_mine_kernel(chips, mine, gi, gs, flat, stage, sems):
    row = lax.axis_index("row")
    put_parts(flat, mine, chips, lax.div(row, 2))
    put_taps(whole_taps(flat, lax.rem(row, 2)), gi, gs, stage, sems)


def unpack_other_kernel(chips, mine, other, gi_in, gs_in, gi, gs, flat, flat_mine, stage, sems):
    del gi_in, gs_in
    row = lax.axis_index("row")
    parity = lax.rem(row, 2)
    put_parts(flat, other, chips, lax.div(row, 2))
    put_parts(flat_mine, mine, chips, lax.div(row, 2))
    taps = whole_taps(flat, 1 - parity)
    half = flat.shape[0]
    cut = half - 4 * 192
    even = parity == 0
    first = jnp.where(even, flat_mine[4 * 192 :, :], flat[4 * 192 :, :])
    second = jnp.where(even, flat[: 192 - cut, :], flat_mine[: 192 - cut, :])
    taps.append((4, jnp.concatenate([first, second], 0)))
    put_taps(taps, gi, gs, stage, sems)


def unpack(mine, other, chips, shape):
    half = mine.shape[0]
    shape = jax.ShapeDtypeStruct((shape[0], shape[2], shape[1]), F32)
    hbm, vmem = pl.BlockSpec(memory_space=pltpu.HBM), pl.BlockSpec(memory_space=pltpu.VMEM)
    flat = pltpu.VMEM((half, 128), F32)

    def stage(count):
        return [pltpu.VMEM((count, 128, 192), F32), pltpu.SemaphoreType.DMA((count, 2))]

    gi, gs = pl.pallas_call(
        functools.partial(unpack_mine_kernel, chips),
        out_shape=(shape, shape),
        out_specs=(hbm, hbm),
        scratch_shapes=[flat] + stage(4),
        compiler_params=mosaic_params(24 * 2**20),
        name="unpack_mine",
    )(mine)
    gi, gs = pl.pallas_call(
        functools.partial(unpack_other_kernel, chips),
        in_specs=[vmem, vmem, hbm, hbm],
        out_shape=(shape, shape),
        out_specs=(hbm, hbm),
        scratch_shapes=[flat, flat] + stage(5),
        input_output_aliases={2: 0, 3: 1},
        compiler_params=mosaic_params(24 * 2**20),
        name="unpack_other",
    )(mine, other, gi, gs)
    return jnp.swapaxes(gi, 1, 2), jnp.swapaxes(gs, 1, 2)


def swaps(nrow, ncol, partner):
    return [
        (r * ncol + c, partner(r, c)[0] * ncol + partner(r, c)[1])
        for r in range(nrow)
        for c in range(ncol)
    ]


def exchanges(nrow, ncol):
    def core(r, c):
        return r ^ 1, c

    def far(r, c):
        if r in (0, nrow - 1):
            return r, c ^ 1
        return r + 1 if r % 2 else r - 1, c

    def even_columns(r, c):
        return r, c ^ 1

    def odd_columns(r, c):
        if c in (0, ncol - 1):
            return r ^ 1, c
        return r, c + 1 if c % 2 else c - 1

    return [swaps(nrow, ncol, f) for f in (core, far, even_columns, odd_columns)]


def local(frames, state, input_weight, state_weight, cotangent):
    ch, tr, tc = state.shape
    nrow, ncol = lax.axis_size("row"), lax.axis_size("col")
    grid = ("row", "col")
    core_pairs, far_pairs, even_pairs, odd_pairs = exchanges(nrow, ncol)
    corners, to_core, *to_far, own, left, right = pack(frames, state, cotangent)
    corners = lax.ppermute(corners, grid, far_pairs)
    nb_core = lax.ppermute(to_core, grid, core_pairs)
    far_a, far_b, far_c = [lax.ppermute(v, grid, far_pairs) for v in to_far]
    wf, wb = arrange_weights(input_weight, state_weight)
    a, b = edges(corners, nb_core, left, right, tr, tc)
    a = lax.ppermute(a, grid, even_pairs)
    b = lax.ppermute(b, grid, odd_pairs)

    chips = nrow // 2
    size = -(-9 * 192 // (nrow * 16)) * 16
    mine, send, p, direct, s2 = main(a, b, own, corners, nb_core, far_a, far_b, far_c, wf, wb, ch, tr, tc, size * nrow)
    got = lax.ppermute(send, grid, core_pairs)
    final, grad, token = finish(p, direct, s2, wb, ch, tr, tc)
    first, *rest = add_core(mine, got, chips)
    masks = sorted(range(1, chips), key=lambda i: (-i.bit_count(), i))
    parts = [
        lax.ppermute(rest[i - 1], "row", [(r, r ^ (2 * i)) for r in range(nrow)]) for i in masks
    ]
    mine = tree_sum([first] + parts, 1.0, "sum_chips", (token,))
    parts = [
        lax.ppermute(mine, "col", [(c, c ^ i) for c in range(ncol)]) for i in range(1, ncol)
    ]
    scale = float((tr * nrow * tc * ncol) ** (-0.5))
    mine = tree_sum([mine] + parts, scale, "sum_col")
    parts = [
        lax.ppermute(mine, "row", [(r, r ^ (2 * i)) for r in range(nrow)])
        for i in range(1, chips)
    ]
    whole = join([mine] + parts)
    other = lax.ppermute(whole, grid, core_pairs)
    gi, gs = unpack(whole, other, chips, input_weight.shape)
    return final, grad, gi, gs


def solution(mesh):
    in_specs = (P(None, None, "row", "col"), P(None, "row", "col"), P(), P(), P(None, "row", "col"))
    out_specs = (P(None, "row", "col"), P(None, "row", "col"), P(), P())
    return jax.shard_map(local, mesh=mesh, in_specs=in_specs, out_specs=out_specs, check_vma=False)
```

```python
import functools

import jax
import jax.numpy as jnp
from jax import lax
from jax.experimental import pallas as pl
from jax.experimental.pallas import tpu as pltpu
from jax.sharding import PartitionSpec as P

F32 = jnp.float32
BF16 = jnp.bfloat16

HALO = 4
EDGE = 4
GAP = 16


def mosaic_params(limit):
    return pltpu.CompilerParams(vmem_limit_bytes=limit)


def pack_kernel(
    tr, tc, fields,
    corners, to_core, to_far_a, to_far_b, to_far_c, own, left, right,
    rows_f32,
):
    ch = fields.shape[0] // 4
    for f, i in enumerate((0, 2, 1, 3)):
        rows_f32[f] = fields[i * ch : (i + 1) * ch].astype(F32).reshape(ch * tr, tc)
    lefts, rights = [], []
    for r in range(tr):
        rows = [rows_f32[f, pl.ds(r, ch, stride=tr), :] for f in range(4)]
        a = jnp.concatenate(rows[:2], 0).T
        b = jnp.concatenate(rows[2:], 0).T
        ab = jnp.concatenate([a, b], 1)
        own[r * tc : (r + 1) * tc, :] = ab.astype(BF16)
        lefts.append(ab[:EDGE])
        rights.append(ab[tc - EDGE :])
    left[...] = jnp.concatenate(lefts, 0).astype(BF16)
    right[...] = jnp.concatenate(rights, 0).astype(BF16)
    parity = lax.rem(lax.axis_index("row"), 2)
    block = HALO * tc
    last = (tr - HALO) * tc
    near = pl.multiple_of((1 - parity) * last, 16)
    far = pl.multiple_of(parity * last, 16)
    to_core[...] = own[pl.ds(near, block), :]
    to_far_a[...] = own[pl.ds(far, block // 2), 0:128]
    to_far_b[...] = own[pl.ds(pl.multiple_of(far + block // 2, 16), block // 2), 0:128]
    to_far_c[...] = own[pl.ds(pl.multiple_of(far + parity * 2 * tc, 16), 2 * tc), 128:256]
    edge = pl.multiple_of(parity * (tr - HALO) * EDGE, 16)
    n = HALO * EDGE
    corners[0:n, :] = left[pl.ds(edge, n), :]
    corners[n : 2 * n, :] = right[pl.ds(edge, n), :]
    third = own[pl.ds(pl.multiple_of(far + (2 - parity) * tc, 16), tc), 128:192].astype(F32)
    q = tc // 4
    corners[2 * n :, :] = jnp.concatenate(
        [third[i * q : (i + 1) * q] for i in range(4)], 1
    ).astype(BF16)


def pack(frames, state, cot):
    ch, tr, tc = state.shape
    edge = jax.ShapeDtypeStruct((tr * EDGE, 4 * ch), BF16)
    return pl.pallas_call(
        functools.partial(pack_kernel, tr, tc),
        out_shape=(
            jax.ShapeDtypeStruct((2 * HALO * EDGE + tc // 4, 4 * ch), BF16),
            jax.ShapeDtypeStruct((HALO * tc, 4 * ch), BF16),
            jax.ShapeDtypeStruct((HALO // 2 * tc, 2 * ch), BF16),
            jax.ShapeDtypeStruct((HALO // 2 * tc, 2 * ch), BF16),
            jax.ShapeDtypeStruct((HALO // 2 * tc, 2 * ch), BF16),
            jax.ShapeDtypeStruct((tr * tc, 4 * ch), BF16),
            edge,
            edge,
        ),
        scratch_shapes=[
            pltpu.VMEM((4, ch * tr, tc), F32),
        ],
        compiler_params=mosaic_params(24 * 2**20),
        name="pack",
    )(jnp.concatenate([frames.reshape(2 * ch, tr, tc), state, cot], 0))


def edges_kernel(tr, tc, nrow, corners, core, left, right, a, b):
    n = HALO * EDGE
    nb = core[...].astype(F32)
    row = lax.axis_index("row")
    has_far = jnp.logical_and(row > 0, row < nrow - 1)
    far = jnp.where(has_far, corners[...].astype(F32), 0.0)
    lefts = [nb[i * tc : i * tc + EDGE] for i in range(HALO)]
    rights = [nb[(i + 1) * tc - EDGE : (i + 1) * tc] for i in range(HALO)]
    lft = jnp.concatenate([left[...].astype(F32)] + lefts + [far[:n]], 0)
    rgt = jnp.concatenate([right[...].astype(F32)] + rights + [far[n : 2 * n]], 0)
    even = lax.rem(lax.axis_index("col"), 2) == 0
    a[...] = jnp.where(even, rgt, lft).astype(BF16)
    b[...] = jnp.where(even, lft, rgt).astype(BF16)


def edges(corners, core, left, right, tr, tc):
    shape = jax.ShapeDtypeStruct(((tr + 2 * HALO) * EDGE, left.shape[1]), BF16)
    return pl.pallas_call(
        functools.partial(edges_kernel, tr, tc, lax.axis_size("row")),
        out_shape=(shape, shape),
        compiler_params=mosaic_params(16 * 2**20),
        name="edges",
    )(corners, core, left, right)


def weights_kernel(iw, sw, so, wf, wb):
    z = jnp.zeros((64, 64), F32)
    for tap in range(9):
        i, s = iw[tap].astype(F32), sw[tap].astype(F32)
        u, r, c = slice(0, 64), slice(64, 128), slice(128, 192)
        at = tap * 128
        wf[at : at + 64, :] = jnp.concatenate([i[:, r], i[:, u], z, i[:, c]], 1).astype(BF16)
        wf[at + 64 : at + 128, :] = jnp.concatenate([s[:, r], s[:, u], s[:, c], z], 1).astype(BF16)
    for dy in range(3):
        back = []
        for dx in range(3):
            s = so[3 * dy + dx].astype(F32)
            back.append(jnp.concatenate([s[r], s[u], s[c], z], 0))
        zb = jnp.zeros((256, 64), F32)
        wb[dy * 256 : (dy + 1) * 256, :] = jnp.concatenate([back[0], back[1], zb, back[2]], 1).astype(BF16)


def arrange_weights(iw, sw):
    return pl.pallas_call(
        weights_kernel,
        out_shape=(jax.ShapeDtypeStruct((1152, 256), BF16), jax.ShapeDtypeStruct((768, 256), BF16)),
        compiler_params=mosaic_params(16 * 2**20),
        name="arrange_weights",
    )(jnp.swapaxes(iw, 1, 2), jnp.swapaxes(sw, 1, 2), sw)


def back_data(p, wb, o, pitch, first, size):
    n = first
    while n < first + size:
        m = min(400, first + size - n)
        x = jnp.concatenate([p[n - k * pitch : n - k * pitch + m, :] for k in (-1, 0, 1)], 1)
        o[n : n + m, :] = jnp.dot(x, wb[...], preferred_element_type=F32)
        n += m


def gathered(o, n, m):
    return (
        pltpu.roll(o[n + 1 : n + 1 + m, 0:128], 64, 1)
        + o[n : n + m, 0:128]
        + o[n - 1 : n - 1 + m, 128:256]
    )


def finish_kernel(tr, tc, p, direct, s2, wb, final_ref, grad_ref, token, o, tmp):
    pitch = tc + GAP
    ch = 64
    for r in range(tr):
        at = (HALO + r) * pitch + GAP
        tmp[pl.ds(r, ch, stride=tr), :] = s2[at : at + tc, :].T[64:, :]
    final_ref[...] = tmp[...].reshape(ch, tr, tc).astype(BF16)
    back_data(p, wb, o, pitch, HALO * pitch, tr * pitch + GAP)
    for r in range(tr):
        at = (HALO + r) * pitch + GAP
        g = direct[at : at + tc, :] + gathered(o, at, tc)
        grad_ref[pl.ds(r, ch, stride=tr), :] = g.T[64:, :]
    token[...] = jnp.zeros(token.shape, F32)


def finish(p, direct, s2, wb, ch, tr, tc):
    final, grad, token = pl.pallas_call(
        functools.partial(finish_kernel, tr, tc),
        out_shape=(
            jax.ShapeDtypeStruct((ch, tr, tc), BF16),
            jax.ShapeDtypeStruct((ch * tr, tc), F32),
            jax.ShapeDtypeStruct((8, 128), F32),
        ),
        scratch_shapes=[
            pltpu.VMEM((p.shape[0], 256), F32),
            pltpu.VMEM((ch * tr, tc), F32),
        ],
        compiler_params=mosaic_params(16 * 2**20),
        name="finish",
    )(p, direct, s2, wb)
    return final, grad.reshape(ch, tr, tc), token


def main_kernel(
    tr, tc, nrow, ncol, flat_rows,
    ea, eb, own, corners, nb_core, far_a, far_b, far_c, wf, wb,
    mine_ref, send_ref, p, direct, s2,
    x1, x2, f2, xd, o, ru1, t1, mask, dw,
):
    pitch = tc + GAP
    ext = tr + 2 * HALO
    total = xd.shape[1]
    pad = 8
    row = lax.axis_index("row")
    col = lax.axis_index("col")
    parity = lax.rem(row, 2)
    lane_low = lax.broadcasted_iota(jnp.int32, (1, 128), 1) < 64

    z8 = jnp.zeros((8, 128), F32)
    for ref in (x1, f2, x2):
        ref[0 : pad + 8, :] = jnp.zeros((pad + 8, 128), F32)
        tail = ref.shape[0] - (pad + ext * pitch + GAP)
        ref[pad + ext * pitch + GAP :, :] = jnp.zeros((tail, 128), F32)
    for r in (0, ext - 1):
        f2[pad + r * pitch + GAP : pad + (r + 1) * pitch, :] = jnp.zeros((tc, 128), F32)

    col_even = lax.rem(col, 2) == 0
    inner = jnp.logical_and(col > 0, col < ncol - 1)
    va, vb = ea[...].astype(F32), jnp.where(inner, eb[...].astype(F32), 0.0)
    lefts, rights = jnp.where(col_even, vb, va), jnp.where(col_even, va, vb)
    lo, hi = slice(0, 128), slice(128, 256)

    def place(ref, start, cells, count):
        for i in range(count):
            at = (start + i) * pitch + pad
            if not isinstance(start, int):
                at = pl.multiple_of(at, 8)
            ref[pl.ds(at + GAP, tc), :] = cells[i * tc : (i + 1) * tc]

    def in_order(v):
        own_rows, core_rows, far_rows = (
            v[: tr * EDGE], v[tr * EDGE : (tr + HALO) * EDGE], v[(tr + HALO) * EDGE :]
        )
        even = parity == 0
        above = jnp.where(even, far_rows, core_rows)
        below = jnp.where(even, core_rows, far_rows)
        return jnp.concatenate([above, own_rows, below], 0)

    lefts, rights = in_order(lefts), in_order(rights)
    none = jnp.zeros((EDGE, 256), F32)
    gap = jnp.zeros((GAP - 2 * EDGE, 256), F32)
    for r in range(ext + 1):
        rgt = rights[(r - 1) * EDGE : r * EDGE] if r > 0 else none
        lft = lefts[r * EDGE : (r + 1) * EDGE] if r < ext else none
        block = jnp.concatenate([rgt, gap, lft], 0)
        x1[pad + r * pitch : pad + r * pitch + GAP, :] = block[:, lo]
        f2[pad + r * pitch : pad + r * pitch + GAP, :] = block[:, hi]

    near = (1 - parity) * (HALO + tr)
    far = parity * (HALO + tr)
    place(x1, HALO, own[:, lo].astype(F32), tr)
    place(f2, HALO, own[:, hi].astype(F32), tr)
    place(x1, near, nb_core[:, lo].astype(F32), HALO)
    place(f2, near, nb_core[:, hi].astype(F32), HALO)
    has_far = jnp.logical_and(row > 0, row < nrow - 1)
    place(x1, far, jnp.where(has_far, far_a[...].astype(F32), 0.0), HALO // 2)
    place(x1, far + HALO // 2, jnp.where(has_far, far_b[...].astype(F32), 0.0), HALO // 2)
    place(f2, far + 2 * (1 - parity), jnp.where(has_far, far_c[...].astype(F32), 0.0), HALO // 2)
    third = jnp.where(has_far, corners[2 * HALO * EDGE :, :].astype(F32), 0.0)
    third = jnp.concatenate([third[:, i * 64 : (i + 1) * 64] for i in range(4)], 0)
    third = jnp.concatenate([third, jnp.zeros((tc, 64), F32)], 1)
    place(f2, far + 1 + parity, third, 1)

    mask[0:8, :] = z8
    tail = mask.shape[0] - (ext * pitch + 8)
    mask[ext * pitch + 8 :, :] = jnp.zeros((tail, 128), F32)
    has_left = (col > 0).astype(F32)
    has_right = (col < ncol - 1).astype(F32)
    for r in range(ext):
        if r < HALO:
            ok = (row > 0).astype(F32)
        elif r >= HALO + tr:
            ok = (row < nrow - 1).astype(F32)
        else:
            ok = jnp.float32(1.0)
        at = r * pitch
        mask[at + 8 : at + GAP, :] = jnp.full((8, 128), ok * has_left, F32)
        mask[at + GAP : at + pitch, :] = jnp.full((tc, 128), ok, F32)
        mask[at + pitch : at + pitch + 8, :] = jnp.full((8, 128), ok * has_right, F32)

    def spread_columns(src, t):
        step = 288
        for n in range(0, total, step):
            m = min(step, total - n)
            for dx in range(3):
                xd[t, n : n + m, dx * 128 : (dx + 1) * 128] = src[
                    pad + n + dx - 1 : pad + n + dx - 1 + m, :
                ].astype(BF16)

    def gates(t, n, m):
        x = jnp.concatenate([xd[t, n + k * pitch : n + k * pitch + m, :] for k in (-1, 0, 1)], 1)
        g = jnp.dot(x, wf[...], preferred_element_type=F32)
        g1, g2 = g[:, :128], g[:, 128:]
        ru = 0.5 * jnp.tanh(0.5 * g1) + 0.5
        c = jnp.tanh(g2 + pltpu.roll(ru * g2, 64, 1))
        return ru, jnp.where(lane_low, g2, c)

    def pre_grads(g, s, ru, tt):
        om = 1.0 - ru
        pc = g * om * (1.0 - tt * tt)
        ph = pltpu.roll(pc, 64, 1) * ru
        pa = jnp.where(lane_low, ph * tt, g * (s - tt) * ru) * om
        pb = jnp.where(lane_low, ph, pc)
        return pa.astype(BF16), pb.astype(BF16)

    spread_columns(x1, 0)
    first = pitch
    m = 128
    count = -(-((ext - 2) * pitch + GAP) // m)
    for i in range(count):
        n = first + i * m
        ru, tt = gates(0, n, m)
        s = x1[pad + n : pad + n + m, :]
        new = (tt + ru * (s - tt)) * mask[n : n + m, :]
        new = new.astype(BF16).astype(F32)
        x2[pad + n : pad + n + m, :] = jnp.where(lane_low, f2[pad + n : pad + n + m, :], new)
        ru1[n : n + m, :] = ru
        t1[n : n + m, :] = tt
    done = first + count * m
    x2[pad + done :, :] = jnp.zeros((x2.shape[0] - pad - done, 128), F32)
    x2[pad + 8 : pad + first, :] = jnp.zeros((first - 8, 128), F32)

    spread_columns(x2, 1)
    first = 2 * pitch
    count = -(-((ext - 4) * pitch + GAP) // m)
    p[0:first, :] = jnp.zeros((first, 256), BF16)
    done = first + count * m
    p[done:, :] = jnp.zeros((p.shape[0] - done, 256), BF16)
    for i in range(count):
        n = first + i * m
        ru, tt = gates(1, n, m)
        s = x2[pad + n : pad + n + m, :]
        s2[n : n + m, :] = tt + ru * (s - tt)
        g = f2[pad + n : pad + n + m, :]
        pa, pb = pre_grads(g, s, ru, tt)
        p[n : n + m, 0:128] = pa
        p[n : n + m, 128:256] = pb
        direct[n : n + m, :] = g * ru
    def weight_grads(t, add):
        pt = jnp.concatenate(
            [
                p[(HALO + r) * pitch + GAP : (HALO + r) * pitch + GAP + tc, :].T
                for r in range(tr)
            ],
            1,
        )
        x = jnp.concatenate(
            [
                jnp.concatenate(
                    [
                        xd[t, (HALO + r + k) * pitch + GAP : (HALO + r + k) * pitch + GAP + tc, :]
                        for k in (-1, 0, 1)
                    ],
                    1,
                )
                for r in range(tr)
            ],
            0,
        )
        d = jnp.dot(pt, x, preferred_element_type=F32)
        dw[...] = dw[...] + d if add else d

    weight_grads(1, False)
    back_data(p, wb, o, pitch, 3 * pitch - 16, (ext - 6) * pitch + 2 * GAP + 96)

    first = 3 * pitch
    m = 256
    count = -(-((ext - 6) * pitch + GAP) // m)
    for i in range(count):
        n = first + i * m
        g = (direct[n : n + m, :] + gathered(o, n, m)) * mask[n : n + m, :]
        ru = ru1[n : n + m, :]
        pa, pb = pre_grads(g, x1[pad + n : pad + n + m, :], ru, t1[n : n + m, :])
        p[n : n + m, 0:128] = pa
        p[n : n + m, 128:256] = pb
        direct[n : n + m, :] = g * ru
    weight_grads(0, True)
    half = flat_rows // 2
    flat = o
    for tap in range(9):
        d = dw[:, tap * 128 : (tap + 1) * 128]
        at = tap * 192
        flat[at : at + 128, 0:128] = d[:128]
        flat[at + 128 : at + 192, 0:128] = jnp.where(lane_low, d[192:256], d[128:192])
    if flat_rows > 9 * 192:
        flat[9 * 192 : flat_rows, 0:128] = jnp.zeros((flat_rows - 9 * 192, 128), F32)
    chips = nrow // 2
    size = half // chips
    chip = lax.div(row, 2)
    for i in range(chips):
        part = jnp.bitwise_xor(chip, i) * size
        at = slice(i * size, (i + 1) * size)
        mine_ref[at, :] = flat[pl.ds(pl.multiple_of(parity * half + part, 16), size), 0:128]
        send_ref[at, :] = flat[
            pl.ds(pl.multiple_of((1 - parity) * half + part, 16), size), 0:128
        ].astype(BF16)


def main(ea, eb, own, corners, nb_core, far_a, far_b, far_c, wf, wb, ch, tr, tc, flat_rows):
    nrow, ncol = lax.axis_size("row"), lax.axis_size("col")
    pitch = tc + GAP
    ext = tr + 2 * HALO
    cells = (ext + 1) * pitch + GAP
    cells = -(-cells // 16) * 16
    o_rows = max(cells, flat_rows)
    half = flat_rows // 2
    return pl.pallas_call(
        functools.partial(main_kernel, tr, tc, nrow, ncol, flat_rows),
        out_shape=(
            jax.ShapeDtypeStruct((half, 128), F32),
            jax.ShapeDtypeStruct((half, 128), BF16),
            jax.ShapeDtypeStruct((cells, 256), BF16),
            jax.ShapeDtypeStruct((cells, 128), F32),
            jax.ShapeDtypeStruct((cells, 128), F32),
        ),
        scratch_shapes=[
            pltpu.VMEM((cells + 16, 128), F32),
            pltpu.VMEM((cells + 16, 128), F32),
            pltpu.VMEM((cells + 16, 128), F32),
            pltpu.VMEM((2, cells, 384), BF16),
            pltpu.VMEM((o_rows, 256), F32),
            pltpu.VMEM((cells, 128), F32),
            pltpu.VMEM((cells, 128), F32),
            pltpu.VMEM((cells, 128), F32),
            pltpu.VMEM((256, 1152), F32),
        ],
        compiler_params=mosaic_params(32 * 2**20),
        cost_estimate=pl.CostEstimate(flops=3000000000, bytes_accessed=4000000, transcendentals=600000),
        name="steps",
    )(ea, eb, own, corners, nb_core, far_a, far_b, far_c, wf, wb)


def add_core_kernel(mine, got, first, *rest):
    size = first.shape[0]
    first[...] = mine[:size] + got[:size].astype(F32)
    for i, ref in enumerate(rest):
        at = slice((i + 1) * size, (i + 2) * size)
        ref[...] = (mine[at] + got[at].astype(F32)).astype(BF16)


def add_core(mine, got, chips):
    size = mine.shape[0] // chips
    part = jax.ShapeDtypeStruct((size, 128), BF16)
    return pl.pallas_call(
        add_core_kernel,
        out_shape=(jax.ShapeDtypeStruct((size, 128), F32),) + (part,) * (chips - 1),
        compiler_params=mosaic_params(16 * 2**20),
        name="add_core",
    )(mine, got)


def tree_sum_kernel(scale, count, *refs):
    values = [r[...].astype(F32) for r in refs[:count]]
    while len(values) > 1:
        values = [values[i] + values[i + 1] for i in range(0, len(values), 2)]
    refs[-1][...] = (values[0] * scale).astype(BF16)


def tree_sum(parts, scale, name, after=()):
    return pl.pallas_call(
        functools.partial(tree_sum_kernel, scale, len(parts)),
        out_shape=jax.ShapeDtypeStruct(parts[0].shape, BF16),
        compiler_params=mosaic_params(16 * 2**20),
        name=name,
    )(*parts, *after)


def join_kernel(*refs):
    size = refs[0].shape[0]
    for i, r in enumerate(refs[:-1]):
        refs[-1][i * size : (i + 1) * size, :] = r[...]


def join(parts):
    size = parts[0].shape[0]
    return pl.pallas_call(
        join_kernel,
        out_shape=jax.ShapeDtypeStruct((size * len(parts), 128), BF16),
        compiler_params=mosaic_params(16 * 2**20),
        name="join",
    )(*parts)


def put_parts(flat, parts, chips, chip):
    size = parts.shape[0] // chips
    for i in range(chips):
        at = pl.multiple_of(jnp.bitwise_xor(chip, i) * size, 16)
        flat[pl.ds(at, size), :] = parts[i * size : (i + 1) * size].astype(F32)


def put_taps(taps, gi, gs, stage, sems):
    copies = []
    for k, (tap, v) in enumerate(taps):
        stage[k] = jnp.concatenate([v[64:128], v[:64], v[128:]], 0).T
        for j, ref in enumerate((gi, gs)):
            copy = pltpu.make_async_copy(
                stage.at[k, pl.ds(j * 64, 64), :], ref.at[tap], sems.at[k, j]
            )
            copy.start()
            copies.append(copy)
    for copy in copies:
        copy.wait()


def whole_taps(flat, parity):
    gap = 5 * 192 - flat.shape[0]
    return [
        (parity * 5 + i, flat[pl.ds(pl.multiple_of(parity * gap + i * 192, 16), 192), :])
        for i in range(4)
    ]


def unpack_mine_kernel(chips, mine, gi, gs, flat, stage, sems):
    row = lax.axis_index("row")
    put_parts(flat, mine, chips, lax.div(row, 2))
    put_taps(whole_taps(flat, lax.rem(row, 2)), gi, gs, stage, sems)


def unpack_other_kernel(chips, mine, other, gi_in, gs_in, gi, gs, flat, flat_mine, stage, sems):
    del gi_in, gs_in
    row = lax.axis_index("row")
    parity = lax.rem(row, 2)
    put_parts(flat, other, chips, lax.div(row, 2))
    put_parts(flat_mine, mine, chips, lax.div(row, 2))
    taps = whole_taps(flat, 1 - parity)
    half = flat.shape[0]
    cut = half - 4 * 192
    even = parity == 0
    first = jnp.where(even, flat_mine[4 * 192 :, :], flat[4 * 192 :, :])
    second = jnp.where(even, flat[: 192 - cut, :], flat_mine[: 192 - cut, :])
    taps.append((4, jnp.concatenate([first, second], 0)))
    put_taps(taps, gi, gs, stage, sems)


def unpack(mine, other, chips, shape):
    half = mine.shape[0]
    shape = jax.ShapeDtypeStruct((shape[0], shape[2], shape[1]), F32)
    hbm, vmem = pl.BlockSpec(memory_space=pltpu.HBM), pl.BlockSpec(memory_space=pltpu.VMEM)
    flat = pltpu.VMEM((half, 128), F32)

    def stage(count):
        return [pltpu.VMEM((count, 128, 192), F32), pltpu.SemaphoreType.DMA((count, 2))]

    gi, gs = pl.pallas_call(
        functools.partial(unpack_mine_kernel, chips),
        out_shape=(shape, shape),
        out_specs=(hbm, hbm),
        scratch_shapes=[flat] + stage(4),
        compiler_params=mosaic_params(24 * 2**20),
        name="unpack_mine",
    )(mine)
    gi, gs = pl.pallas_call(
        functools.partial(unpack_other_kernel, chips),
        in_specs=[vmem, vmem, hbm, hbm],
        out_shape=(shape, shape),
        out_specs=(hbm, hbm),
        scratch_shapes=[flat, flat] + stage(5),
        input_output_aliases={2: 0, 3: 1},
        compiler_params=mosaic_params(24 * 2**20),
        name="unpack_other",
    )(mine, other, gi, gs)
    return jnp.swapaxes(gi, 1, 2), jnp.swapaxes(gs, 1, 2)


def swaps(nrow, ncol, partner):
    return [
        (r * ncol + c, partner(r, c)[0] * ncol + partner(r, c)[1])
        for r in range(nrow)
        for c in range(ncol)
    ]


def exchanges(nrow, ncol):
    def core(r, c):
        return r ^ 1, c

    def far(r, c):
        if r in (0, nrow - 1):
            return r, c ^ 1
        return r + 1 if r % 2 else r - 1, c

    def even_columns(r, c):
        return r, c ^ 1

    def odd_columns(r, c):
        if c in (0, ncol - 1):
            return r ^ 1, c
        return r, c + 1 if c % 2 else c - 1

    return [swaps(nrow, ncol, f) for f in (core, far, even_columns, odd_columns)]


def local(frames, state, input_weight, state_weight, cotangent):
    ch, tr, tc = state.shape
    nrow, ncol = lax.axis_size("row"), lax.axis_size("col")
    grid = ("row", "col")
    core_pairs, far_pairs, even_pairs, odd_pairs = exchanges(nrow, ncol)
    corners, to_core, *to_far, own, left, right = pack(frames, state, cotangent)
    corners = lax.ppermute(corners, grid, far_pairs)
    nb_core = lax.ppermute(to_core, grid, core_pairs)
    far_a, far_b, far_c = [lax.ppermute(v, grid, far_pairs) for v in to_far]
    wf, wb = arrange_weights(input_weight, state_weight)
    a, b = edges(corners, nb_core, left, right, tr, tc)
    a = lax.ppermute(a, grid, even_pairs)
    b = lax.ppermute(b, grid, odd_pairs)

    chips = nrow // 2
    size = -(-9 * 192 // (nrow * 16)) * 16
    mine, send, p, direct, s2 = main(a, b, own, corners, nb_core, far_a, far_b, far_c, wf, wb, ch, tr, tc, size * nrow)
    got = lax.ppermute(send, grid, core_pairs)
    final, grad, token = finish(p, direct, s2, wb, ch, tr, tc)
    first, *rest = add_core(mine, got, chips)
    masks = sorted(range(1, chips), key=lambda i: (-i.bit_count(), i))
    parts = [
        lax.ppermute(rest[i - 1], "row", [(r, r ^ (2 * i)) for r in range(nrow)]) for i in masks
    ]
    mine = tree_sum([first] + parts, 1.0, "sum_chips", (token,))
    parts = [
        lax.ppermute(mine, "col", [(c, c ^ i) for c in range(ncol)]) for i in range(1, ncol)
    ]
    scale = float((tr * nrow * tc * ncol) ** (-0.5))
    mine = tree_sum([mine] + parts, scale, "sum_col")
    parts = [
        lax.ppermute(mine, "row", [(r, r ^ (2 * i)) for r in range(nrow)])
        for i in range(1, chips)
    ]
    whole = join([mine] + parts)
    other = lax.ppermute(whole, grid, core_pairs)
    gi, gs = unpack(whole, other, chips, input_weight.shape)
    return final, grad, gi, gs


def solution(mesh):
    in_specs = (P(None, None, "row", "col"), P(None, "row", "col"), P(), P(), P(None, "row", "col"))
    out_specs = (P(None, "row", "col"), P(None, "row", "col"), P(), P())
    return jax.shard_map(local, mesh=mesh, in_specs=in_specs, out_specs=out_specs, check_vma=False)
```

```python
import functools

import jax
import jax.numpy as jnp
from jax import lax
from jax.experimental import pallas as pl
from jax.experimental.pallas import tpu as pltpu
from jax.sharding import PartitionSpec as P

F32 = jnp.float32
BF16 = jnp.bfloat16

HALO = 4
EDGE = 4
GAP = 16


def mosaic_params(limit):
    return pltpu.CompilerParams(vmem_limit_bytes=limit)


def pack_kernel(
    tr, tc, fields,
    corners, to_core, to_far_a, to_far_b, to_far_c, own, left, right,
    rows_f32,
):
    ch = fields.shape[0] // 4
    for f, i in enumerate((0, 2, 1, 3)):
        rows_f32[f] = fields[i * ch : (i + 1) * ch].astype(F32).reshape(ch * tr, tc)
    lefts, rights = [], []
    for r in range(tr):
        rows = [rows_f32[f, pl.ds(r, ch, stride=tr), :] for f in range(4)]
        a = jnp.concatenate(rows[:2], 0).T
        b = jnp.concatenate(rows[2:], 0).T
        ab = jnp.concatenate([a, b], 1)
        own[r * tc : (r + 1) * tc, :] = ab.astype(BF16)
        lefts.append(ab[:EDGE])
        rights.append(ab[tc - EDGE :])
    left[...] = jnp.concatenate(lefts, 0).astype(BF16)
    right[...] = jnp.concatenate(rights, 0).astype(BF16)
    parity = lax.rem(lax.axis_index("row"), 2)
    block = HALO * tc
    last = (tr - HALO) * tc
    near = pl.multiple_of((1 - parity) * last, 16)
    far = pl.multiple_of(parity * last, 16)
    to_core[...] = own[pl.ds(near, block), :]
    to_far_a[...] = own[pl.ds(far, block // 2), 0:128]
    to_far_b[...] = own[pl.ds(pl.multiple_of(far + block // 2, 16), block // 2), 0:128]
    to_far_c[...] = own[pl.ds(pl.multiple_of(far + parity * 2 * tc, 16), 2 * tc), 128:256]
    edge = pl.multiple_of(parity * (tr - HALO) * EDGE, 16)
    n = HALO * EDGE
    corners[0:n, :] = left[pl.ds(edge, n), :]
    corners[n : 2 * n, :] = right[pl.ds(edge, n), :]
    third = own[pl.ds(pl.multiple_of(far + (2 - parity) * tc, 16), tc), 128:192].astype(F32)
    q = tc // 4
    corners[2 * n :, :] = jnp.concatenate(
        [third[i * q : (i + 1) * q] for i in range(4)], 1
    ).astype(BF16)


def pack(frames, state, cot):
    ch, tr, tc = state.shape
    edge = jax.ShapeDtypeStruct((tr * EDGE, 4 * ch), BF16)
    return pl.pallas_call(
        functools.partial(pack_kernel, tr, tc),
        out_shape=(
            jax.ShapeDtypeStruct((2 * HALO * EDGE + tc // 4, 4 * ch), BF16),
            jax.ShapeDtypeStruct((HALO * tc, 4 * ch), BF16),
            jax.ShapeDtypeStruct((HALO // 2 * tc, 2 * ch), BF16),
            jax.ShapeDtypeStruct((HALO // 2 * tc, 2 * ch), BF16),
            jax.ShapeDtypeStruct((HALO // 2 * tc, 2 * ch), BF16),
            jax.ShapeDtypeStruct((tr * tc, 4 * ch), BF16),
            edge,
            edge,
        ),
        scratch_shapes=[
            pltpu.VMEM((4, ch * tr, tc), F32),
        ],
        compiler_params=mosaic_params(24 * 2**20),
        name="pack",
    )(jnp.concatenate([frames.reshape(2 * ch, tr, tc), state, cot], 0))


def edges_kernel(tr, tc, nrow, corners, core, left, right, a, b):
    n = HALO * EDGE
    nb = core[...].astype(F32)
    row = lax.axis_index("row")
    has_far = jnp.logical_and(row > 0, row < nrow - 1)
    far = jnp.where(has_far, corners[...].astype(F32), 0.0)
    lefts = [nb[i * tc : i * tc + EDGE] for i in range(HALO)]
    rights = [nb[(i + 1) * tc - EDGE : (i + 1) * tc] for i in range(HALO)]
    lft = jnp.concatenate([left[...].astype(F32)] + lefts + [far[:n]], 0)
    rgt = jnp.concatenate([right[...].astype(F32)] + rights + [far[n : 2 * n]], 0)
    even = lax.rem(lax.axis_index("col"), 2) == 0
    a[...] = jnp.where(even, rgt, lft).astype(BF16)
    b[...] = jnp.where(even, lft, rgt).astype(BF16)


def edges(corners, core, left, right, tr, tc):
    shape = jax.ShapeDtypeStruct(((tr + 2 * HALO) * EDGE, left.shape[1]), BF16)
    return pl.pallas_call(
        functools.partial(edges_kernel, tr, tc, lax.axis_size("row")),
        out_shape=(shape, shape),
        compiler_params=mosaic_params(16 * 2**20),
        name="edges",
    )(corners, core, left, right)


def weights_kernel(iw, sw, wf, wb):
    z = jnp.zeros((64, 64), F32)
    for tap in range(9):
        i, s = iw[tap].astype(F32), sw[tap].astype(F32)
        u, r, c = slice(0, 64), slice(64, 128), slice(128, 192)
        at = tap * 128
        wf[at : at + 64, :] = jnp.concatenate([i[:, r], i[:, u], z, i[:, c]], 1).astype(BF16)
        wf[at + 64 : at + 128, :] = jnp.concatenate([s[:, r], s[:, u], s[:, c], z], 1).astype(BF16)
    for dy in range(3):
        back = []
        for dx in range(3):
            s = sw[3 * dy + dx].astype(F32)
            back.append(jnp.concatenate([s[:, r], s[:, u], s[:, c], z], 1).T)
        zb = jnp.zeros((256, 64), F32)
        wb[dy * 256 : (dy + 1) * 256, :] = jnp.concatenate([back[0], back[1], zb, back[2]], 1).astype(BF16)


def arrange_weights(iw, sw):
    return pl.pallas_call(
        weights_kernel,
        out_shape=(jax.ShapeDtypeStruct((1152, 256), BF16), jax.ShapeDtypeStruct((768, 256), BF16)),
        compiler_params=mosaic_params(16 * 2**20),
        name="arrange_weights",
    )(jnp.swapaxes(iw, 1, 2), jnp.swapaxes(sw, 1, 2))


def back_data(p, wb, o, pitch, first, size):
    n = first
    while n < first + size:
        m = min(400, first + size - n)
        x = jnp.concatenate([p[n - k * pitch : n - k * pitch + m, :] for k in (-1, 0, 1)], 1)
        o[n : n + m, :] = jnp.dot(x, wb[...], preferred_element_type=F32)
        n += m


def gathered(o, n, m):
    return (
        pltpu.roll(o[n + 1 : n + 1 + m, 0:128], 64, 1)
        + o[n : n + m, 0:128]
        + o[n - 1 : n - 1 + m, 128:256]
    )


def finish_kernel(tr, tc, p, direct, s2, wb, final_ref, grad_ref, token, o, tmp):
    pitch = tc + GAP
    ch = 64
    for r in range(tr):
        at = (HALO + r) * pitch + GAP
        tmp[pl.ds(r, ch, stride=tr), :] = s2[at : at + tc, :].T[64:, :]
    final_ref[...] = tmp[...].reshape(ch, tr, tc).astype(BF16)
    back_data(p, wb, o, pitch, HALO * pitch, tr * pitch + GAP)
    for r in range(tr):
        at = (HALO + r) * pitch + GAP
        g = direct[at : at + tc, :] + gathered(o, at, tc)
        grad_ref[pl.ds(r, ch, stride=tr), :] = g.T[64:, :]
    token[...] = jnp.zeros(token.shape, F32)


def finish(p, direct, s2, wb, ch, tr, tc):
    final, grad, token = pl.pallas_call(
        functools.partial(finish_kernel, tr, tc),
        out_shape=(
            jax.ShapeDtypeStruct((ch, tr, tc), BF16),
            jax.ShapeDtypeStruct((ch * tr, tc), F32),
            jax.ShapeDtypeStruct((8, 128), F32),
        ),
        scratch_shapes=[
            pltpu.VMEM((p.shape[0], 256), F32),
            pltpu.VMEM((ch * tr, tc), F32),
        ],
        compiler_params=mosaic_params(16 * 2**20),
        name="finish",
    )(p, direct, s2, wb)
    return final, grad.reshape(ch, tr, tc), token


def main_kernel(
    tr, tc, nrow, ncol, flat_rows,
    ea, eb, own, corners, nb_core, far_a, far_b, far_c, wf, wb,
    mine_ref, send_ref, p, direct, s2,
    x1, x2, f2, xd, o, ru1, t1, mask, dw,
):
    pitch = tc + GAP
    ext = tr + 2 * HALO
    total = xd.shape[1]
    pad = 8
    row = lax.axis_index("row")
    col = lax.axis_index("col")
    parity = lax.rem(row, 2)
    lane_low = lax.broadcasted_iota(jnp.int32, (1, 128), 1) < 64

    z8 = jnp.zeros((8, 128), F32)
    for ref in (x1, f2, x2):
        ref[0 : pad + 8, :] = jnp.zeros((pad + 8, 128), F32)
        tail = ref.shape[0] - (pad + ext * pitch + GAP)
        ref[pad + ext * pitch + GAP :, :] = jnp.zeros((tail, 128), F32)
    for r in (0, ext - 1):
        f2[pad + r * pitch + GAP : pad + (r + 1) * pitch, :] = jnp.zeros((tc, 128), F32)

    col_even = lax.rem(col, 2) == 0
    inner = jnp.logical_and(col > 0, col < ncol - 1)
    va, vb = ea[...].astype(F32), jnp.where(inner, eb[...].astype(F32), 0.0)
    lefts, rights = jnp.where(col_even, vb, va), jnp.where(col_even, va, vb)
    lo, hi = slice(0, 128), slice(128, 256)

    def place(ref, start, cells, count):
        for i in range(count):
            at = (start + i) * pitch + pad
            if not isinstance(start, int):
                at = pl.multiple_of(at, 8)
            ref[pl.ds(at + GAP, tc), :] = cells[i * tc : (i + 1) * tc]

    def in_order(v):
        own_rows, core_rows, far_rows = (
            v[: tr * EDGE], v[tr * EDGE : (tr + HALO) * EDGE], v[(tr + HALO) * EDGE :]
        )
        even = parity == 0
        above = jnp.where(even, far_rows, core_rows)
        below = jnp.where(even, core_rows, far_rows)
        return jnp.concatenate([above, own_rows, below], 0)

    lefts, rights = in_order(lefts), in_order(rights)
    none = jnp.zeros((EDGE, 256), F32)
    gap = jnp.zeros((GAP - 2 * EDGE, 256), F32)
    for r in range(ext + 1):
        rgt = rights[(r - 1) * EDGE : r * EDGE] if r > 0 else none
        lft = lefts[r * EDGE : (r + 1) * EDGE] if r < ext else none
        block = jnp.concatenate([rgt, gap, lft], 0)
        x1[pad + r * pitch : pad + r * pitch + GAP, :] = block[:, lo]
        f2[pad + r * pitch : pad + r * pitch + GAP, :] = block[:, hi]

    near = (1 - parity) * (HALO + tr)
    far = parity * (HALO + tr)
    place(x1, HALO, own[:, lo].astype(F32), tr)
    place(f2, HALO, own[:, hi].astype(F32), tr)
    place(x1, near, nb_core[:, lo].astype(F32), HALO)
    place(f2, near, nb_core[:, hi].astype(F32), HALO)
    has_far = jnp.logical_and(row > 0, row < nrow - 1)
    place(x1, far, jnp.where(has_far, far_a[...].astype(F32), 0.0), HALO // 2)
    place(x1, far + HALO // 2, jnp.where(has_far, far_b[...].astype(F32), 0.0), HALO // 2)
    place(f2, far + 2 * (1 - parity), jnp.where(has_far, far_c[...].astype(F32), 0.0), HALO // 2)
    third = jnp.where(has_far, corners[2 * HALO * EDGE :, :].astype(F32), 0.0)
    third = jnp.concatenate([third[:, i * 64 : (i + 1) * 64] for i in range(4)], 0)
    third = jnp.concatenate([third, jnp.zeros((tc, 64), F32)], 1)
    place(f2, far + 1 + parity, third, 1)

    mask[0:8, :] = z8
    tail = mask.shape[0] - (ext * pitch + 8)
    mask[ext * pitch + 8 :, :] = jnp.zeros((tail, 128), F32)
    has_left = (col > 0).astype(F32)
    has_right = (col < ncol - 1).astype(F32)
    for r in range(ext):
        if r < HALO:
            ok = (row > 0).astype(F32)
        elif r >= HALO + tr:
            ok = (row < nrow - 1).astype(F32)
        else:
            ok = jnp.float32(1.0)
        at = r * pitch
        mask[at + 8 : at + GAP, :] = jnp.full((8, 128), ok * has_left, F32)
        mask[at + GAP : at + pitch, :] = jnp.full((tc, 128), ok, F32)
        mask[at + pitch : at + pitch + 8, :] = jnp.full((8, 128), ok * has_right, F32)

    def spread_columns(src, t):
        step = 288
        for n in range(0, total, step):
            m = min(step, total - n)
            for dx in range(3):
                xd[t, n : n + m, dx * 128 : (dx + 1) * 128] = src[
                    pad + n + dx - 1 : pad + n + dx - 1 + m, :
                ].astype(BF16)

    def gates(t, n, m):
        x = jnp.concatenate([xd[t, n + k * pitch : n + k * pitch + m, :] for k in (-1, 0, 1)], 1)
        g = jnp.dot(x, wf[...], preferred_element_type=F32)
        g1, g2 = g[:, :128], g[:, 128:]
        ru = 0.5 * jnp.tanh(0.5 * g1) + 0.5
        c = jnp.tanh(g2 + pltpu.roll(ru * g2, 64, 1))
        return ru, jnp.where(lane_low, g2, c)

    def pre_grads(g, s, ru, tt):
        om = 1.0 - ru
        pc = g * om * (1.0 - tt * tt)
        ph = pltpu.roll(pc, 64, 1) * ru
        pa = jnp.where(lane_low, ph * tt, g * (s - tt) * ru) * om
        pb = jnp.where(lane_low, ph, pc)
        return pa.astype(BF16), pb.astype(BF16)

    spread_columns(x1, 0)
    first = pitch
    m = 128
    count = -(-((ext - 2) * pitch + GAP) // m)
    for i in range(count):
        n = first + i * m
        ru, tt = gates(0, n, m)
        s = x1[pad + n : pad + n + m, :]
        new = (tt + ru * (s - tt)) * mask[n : n + m, :]
        new = new.astype(BF16).astype(F32)
        x2[pad + n : pad + n + m, :] = jnp.where(lane_low, f2[pad + n : pad + n + m, :], new)
        ru1[n : n + m, :] = ru
        t1[n : n + m, :] = tt
    done = first + count * m
    x2[pad + done :, :] = jnp.zeros((x2.shape[0] - pad - done, 128), F32)
    x2[pad + 8 : pad + first, :] = jnp.zeros((first - 8, 128), F32)

    spread_columns(x2, 1)
    first = 2 * pitch
    count = -(-((ext - 4) * pitch + GAP) // m)
    p[0:first, :] = jnp.zeros((first, 256), BF16)
    done = first + count * m
    p[done:, :] = jnp.zeros((p.shape[0] - done, 256), BF16)
    for i in range(count):
        n = first + i * m
        ru, tt = gates(1, n, m)
        s = x2[pad + n : pad + n + m, :]
        s2[n : n + m, :] = tt + ru * (s - tt)
        g = f2[pad + n : pad + n + m, :]
        pa, pb = pre_grads(g, s, ru, tt)
        p[n : n + m, 0:128] = pa
        p[n : n + m, 128:256] = pb
        direct[n : n + m, :] = g * ru
    def weight_grads(t, add):
        pt = jnp.concatenate(
            [
                p[(HALO + r) * pitch + GAP : (HALO + r) * pitch + GAP + tc, :].T
                for r in range(tr)
            ],
            1,
        )
        x = jnp.concatenate(
            [
                jnp.concatenate(
                    [
                        xd[t, (HALO + r + k) * pitch + GAP : (HALO + r + k) * pitch + GAP + tc, :]
                        for k in (-1, 0, 1)
                    ],
                    1,
                )
                for r in range(tr)
            ],
            0,
        )
        d = jnp.dot(pt, x, preferred_element_type=F32)
        dw[...] = dw[...] + d if add else d

    weight_grads(1, False)
    back_data(p, wb, o, pitch, 3 * pitch - 16, (ext - 6) * pitch + 2 * GAP + 96)

    first = 3 * pitch
    count = -(-((ext - 6) * pitch + GAP) // m)
    for i in range(count):
        n = first + i * m
        g = (direct[n : n + m, :] + gathered(o, n, m)) * mask[n : n + m, :]
        ru = ru1[n : n + m, :]
        pa, pb = pre_grads(g, x1[pad + n : pad + n + m, :], ru, t1[n : n + m, :])
        p[n : n + m, 0:128] = pa
        p[n : n + m, 128:256] = pb
        direct[n : n + m, :] = g * ru
    weight_grads(0, True)
    half = flat_rows // 2
    flat = o
    for tap in range(9):
        d = dw[:, tap * 128 : (tap + 1) * 128]
        at = tap * 192
        flat[at : at + 128, 0:128] = d[:128]
        flat[at + 128 : at + 192, 0:128] = jnp.where(lane_low, d[192:256], d[128:192])
    if flat_rows > 9 * 192:
        flat[9 * 192 : flat_rows, 0:128] = jnp.zeros((flat_rows - 9 * 192, 128), F32)
    chips = nrow // 2
    size = half // chips
    chip = lax.div(row, 2)
    for i in range(chips):
        part = jnp.bitwise_xor(chip, i) * size
        at = slice(i * size, (i + 1) * size)
        mine_ref[at, :] = flat[pl.ds(pl.multiple_of(parity * half + part, 16), size), 0:128]
        send_ref[at, :] = flat[
            pl.ds(pl.multiple_of((1 - parity) * half + part, 16), size), 0:128
        ].astype(BF16)


def main(ea, eb, own, corners, nb_core, far_a, far_b, far_c, wf, wb, ch, tr, tc, flat_rows):
    nrow, ncol = lax.axis_size("row"), lax.axis_size("col")
    pitch = tc + GAP
    ext = tr + 2 * HALO
    cells = (ext + 1) * pitch + GAP
    cells = -(-cells // 16) * 16
    o_rows = max(cells, flat_rows)
    half = flat_rows // 2
    return pl.pallas_call(
        functools.partial(main_kernel, tr, tc, nrow, ncol, flat_rows),
        out_shape=(
            jax.ShapeDtypeStruct((half, 128), F32),
            jax.ShapeDtypeStruct((half, 128), BF16),
            jax.ShapeDtypeStruct((cells, 256), BF16),
            jax.ShapeDtypeStruct((cells, 128), F32),
            jax.ShapeDtypeStruct((cells, 128), F32),
        ),
        scratch_shapes=[
            pltpu.VMEM((cells + 16, 128), F32),
            pltpu.VMEM((cells + 16, 128), F32),
            pltpu.VMEM((cells + 16, 128), F32),
            pltpu.VMEM((2, cells, 384), BF16),
            pltpu.VMEM((o_rows, 256), F32),
            pltpu.VMEM((cells, 128), F32),
            pltpu.VMEM((cells, 128), F32),
            pltpu.VMEM((cells, 128), F32),
            pltpu.VMEM((256, 1152), F32),
        ],
        compiler_params=mosaic_params(32 * 2**20),
        cost_estimate=pl.CostEstimate(flops=3000000000, bytes_accessed=4000000, transcendentals=600000),
        name="steps",
    )(ea, eb, own, corners, nb_core, far_a, far_b, far_c, wf, wb)


def add_core_kernel(mine, got, first, *rest):
    size = first.shape[0]
    first[...] = mine[:size] + got[:size].astype(F32)
    for i, ref in enumerate(rest):
        at = slice((i + 1) * size, (i + 2) * size)
        ref[...] = (mine[at] + got[at].astype(F32)).astype(BF16)


def add_core(mine, got, chips):
    size = mine.shape[0] // chips
    part = jax.ShapeDtypeStruct((size, 128), BF16)
    return pl.pallas_call(
        add_core_kernel,
        out_shape=(jax.ShapeDtypeStruct((size, 128), F32),) + (part,) * (chips - 1),
        compiler_params=mosaic_params(16 * 2**20),
        name="add_core",
    )(mine, got)


def tree_sum_kernel(scale, count, *refs):
    values = [r[...].astype(F32) for r in refs[:count]]
    while len(values) > 1:
        values = [values[i] + values[i + 1] for i in range(0, len(values), 2)]
    refs[-1][...] = (values[0] * scale).astype(BF16)


def tree_sum(parts, scale, name, after=()):
    return pl.pallas_call(
        functools.partial(tree_sum_kernel, scale, len(parts)),
        out_shape=jax.ShapeDtypeStruct(parts[0].shape, BF16),
        compiler_params=mosaic_params(16 * 2**20),
        name=name,
    )(*parts, *after)


def join_kernel(*refs):
    size = refs[0].shape[0]
    for i, r in enumerate(refs[:-1]):
        refs[-1][i * size : (i + 1) * size, :] = r[...]


def join(parts):
    size = parts[0].shape[0]
    return pl.pallas_call(
        join_kernel,
        out_shape=jax.ShapeDtypeStruct((size * len(parts), 128), BF16),
        compiler_params=mosaic_params(16 * 2**20),
        name="join",
    )(*parts)


def put_parts(flat, parts, chips, chip):
    size = parts.shape[0] // chips
    for i in range(chips):
        at = pl.multiple_of(jnp.bitwise_xor(chip, i) * size, 16)
        flat[pl.ds(at, size), :] = parts[i * size : (i + 1) * size].astype(F32)


def put_taps(taps, gi, gs, stage, sems):
    copies = []
    for k, (tap, v) in enumerate(taps):
        stage[k] = jnp.concatenate([v[64:128], v[:64], v[128:]], 0).T
        for j, ref in enumerate((gi, gs)):
            copy = pltpu.make_async_copy(
                stage.at[k, pl.ds(j * 64, 64), :], ref.at[tap], sems.at[k, j]
            )
            copy.start()
            copies.append(copy)
    for copy in copies:
        copy.wait()


def whole_taps(flat, parity):
    gap = 5 * 192 - flat.shape[0]
    return [
        (parity * 5 + i, flat[pl.ds(pl.multiple_of(parity * gap + i * 192, 16), 192), :])
        for i in range(4)
    ]


def unpack_mine_kernel(chips, mine, gi, gs, flat, stage, sems):
    row = lax.axis_index("row")
    put_parts(flat, mine, chips, lax.div(row, 2))
    put_taps(whole_taps(flat, lax.rem(row, 2)), gi, gs, stage, sems)


def unpack_other_kernel(chips, mine, other, gi_in, gs_in, gi, gs, flat, flat_mine, stage, sems):
    del gi_in, gs_in
    row = lax.axis_index("row")
    parity = lax.rem(row, 2)
    put_parts(flat, other, chips, lax.div(row, 2))
    put_parts(flat_mine, mine, chips, lax.div(row, 2))
    taps = whole_taps(flat, 1 - parity)
    half = flat.shape[0]
    cut = half - 4 * 192
    even = parity == 0
    first = jnp.where(even, flat_mine[4 * 192 :, :], flat[4 * 192 :, :])
    second = jnp.where(even, flat[: 192 - cut, :], flat_mine[: 192 - cut, :])
    taps.append((4, jnp.concatenate([first, second], 0)))
    put_taps(taps, gi, gs, stage, sems)


def unpack(mine, other, chips, shape):
    half = mine.shape[0]
    shape = jax.ShapeDtypeStruct((shape[0], shape[2], shape[1]), F32)
    hbm, vmem = pl.BlockSpec(memory_space=pltpu.HBM), pl.BlockSpec(memory_space=pltpu.VMEM)
    flat = pltpu.VMEM((half, 128), F32)

    def stage(count):
        return [pltpu.VMEM((count, 128, 192), F32), pltpu.SemaphoreType.DMA((count, 2))]

    gi, gs = pl.pallas_call(
        functools.partial(unpack_mine_kernel, chips),
        out_shape=(shape, shape),
        out_specs=(hbm, hbm),
        scratch_shapes=[flat] + stage(4),
        compiler_params=mosaic_params(24 * 2**20),
        name="unpack_mine",
    )(mine)
    gi, gs = pl.pallas_call(
        functools.partial(unpack_other_kernel, chips),
        in_specs=[vmem, vmem, hbm, hbm],
        out_shape=(shape, shape),
        out_specs=(hbm, hbm),
        scratch_shapes=[flat, flat] + stage(5),
        input_output_aliases={2: 0, 3: 1},
        compiler_params=mosaic_params(24 * 2**20),
        name="unpack_other",
    )(mine, other, gi, gs)
    return jnp.swapaxes(gi, 1, 2), jnp.swapaxes(gs, 1, 2)


def swaps(nrow, ncol, partner):
    return [
        (r * ncol + c, partner(r, c)[0] * ncol + partner(r, c)[1])
        for r in range(nrow)
        for c in range(ncol)
    ]


def exchanges(nrow, ncol):
    def core(r, c):
        return r ^ 1, c

    def far(r, c):
        if r in (0, nrow - 1):
            return r, c ^ 1
        return r + 1 if r % 2 else r - 1, c

    def even_columns(r, c):
        return r, c ^ 1

    def odd_columns(r, c):
        if c in (0, ncol - 1):
            return r ^ 1, c
        return r, c + 1 if c % 2 else c - 1

    return [swaps(nrow, ncol, f) for f in (core, far, even_columns, odd_columns)]


def local(frames, state, input_weight, state_weight, cotangent):
    ch, tr, tc = state.shape
    nrow, ncol = lax.axis_size("row"), lax.axis_size("col")
    grid = ("row", "col")
    core_pairs, far_pairs, even_pairs, odd_pairs = exchanges(nrow, ncol)
    corners, to_core, *to_far, own, left, right = pack(frames, state, cotangent)
    corners = lax.ppermute(corners, grid, far_pairs)
    nb_core = lax.ppermute(to_core, grid, core_pairs)
    far_a, far_b, far_c = [lax.ppermute(v, grid, far_pairs) for v in to_far]
    wf, wb = arrange_weights(input_weight, state_weight)
    a, b = edges(corners, nb_core, left, right, tr, tc)
    a = lax.ppermute(a, grid, even_pairs)
    b = lax.ppermute(b, grid, odd_pairs)

    chips = nrow // 2
    size = -(-9 * 192 // (nrow * 16)) * 16
    mine, send, p, direct, s2 = main(a, b, own, corners, nb_core, far_a, far_b, far_c, wf, wb, ch, tr, tc, size * nrow)
    got = lax.ppermute(send, grid, core_pairs)
    final, grad, token = finish(p, direct, s2, wb, ch, tr, tc)
    first, *rest = add_core(mine, got, chips)
    masks = sorted(range(1, chips), key=lambda i: (-i.bit_count(), i))
    parts = [
        lax.ppermute(rest[i - 1], "row", [(r, r ^ (2 * i)) for r in range(nrow)]) for i in masks
    ]
    mine = tree_sum([first] + parts, 1.0, "sum_chips")
    parts = [
        lax.ppermute(mine, "col", [(c, c ^ i) for c in range(ncol)]) for i in range(1, ncol)
    ]
    scale = float((tr * nrow * tc * ncol) ** (-0.5))
    mine = tree_sum([mine] + parts, scale, "sum_col", (token,))
    parts = [
        lax.ppermute(mine, "row", [(r, r ^ (2 * i)) for r in range(nrow)])
        for i in range(1, chips)
    ]
    whole = join([mine] + parts)
    other = lax.ppermute(whole, grid, core_pairs)
    gi, gs = unpack(whole, other, chips, input_weight.shape)
    return final, grad, gi, gs


def solution(mesh):
    in_specs = (P(None, None, "row", "col"), P(None, "row", "col"), P(), P(), P(None, "row", "col"))
    out_specs = (P(None, "row", "col"), P(None, "row", "col"), P(), P())
    return jax.shard_map(local, mesh=mesh, in_specs=in_specs, out_specs=out_specs, check_vma=False)
```
